128 devices in a mesh: own: 16 (over x, z), help: 8 (over y, core).
Axes of the slice: x: 4, y: 4, z: 4, core: 2. Of those that a mesh axis runs over, the one named last changes fastest.
Arguments:
- points: bfloat16 [524288, 1024], P(('own', 'help')), may hold values from -64 to 64
- cluster_of: int32 [524288, 1], P(('own', 'help')), may hold values from 0 to 63; in each aligned block of 4096 rows (0 to 4095, 4096 to 8191, ...) at most 80 rows name the same one
- sub_init: int32 [524288], P(('own', 'help')), may hold values from 0 to 63
Outputs:
- centroids: float32 [64, 64, 1024], P(None, 'own')
The draws below stay inside these ranges and needn't reach their ends.
Inputs may be any that keep to these rules, and one draw needn't show every extreme that they name: `cluster_of`: among the 4096 rows of one device no cluster appears more than 80 times; some cluster appears exactly 80 times in some device's rows.
All inputs are finite; a program needn't handle non-finite values.
Results may differ from the reference program's by a relative error of at most 0.04.
The reference program's roundings to bfloat16 on the way count: a program that leaves them out, or rounds other values in their place, can miss the bound.
Values may be sent and summed in bfloat16 or wider, within the bound.
A program may use at most 128 MiB of HBM per device.

```python
import math
import jax
import jax.numpy as jnp
import numpy as np
from jax import lax

D = 1024
SUB = 64
ITERS = 3
P_DEV = 4096
CLUSTERS = 64
MOST = 80
POINTS = 524288


def draw_points(key, part):
    key = jax.random.fold_in(key, 11)
    base = jax.random.normal(jax.random.fold_in(key, 1), (POINTS, D), jnp.float32)
    return jnp.clip(base, -64.0, 64.0).astype(jnp.bfloat16)


def with_ends(array, own_key, smallest, largest):
    extent = array.shape
    place = [jax.random.randint(jax.random.fold_in(own_key, axis), (), 0, extent[axis]) for axis in range(len(extent))]
    array = array.at[tuple(place)].set(smallest)
    longest = extent.index(max(extent))
    place[longest] = (place[longest] + 1) % extent[longest]
    return array.at[tuple(place)].set(largest)


def assign_block(key, own, number, rows, count, top, most, slope):
    order = jax.random.permutation(key, count)
    crowded, usual = shares(count, rows * top, most, slope, True), shares(count, rows * top, most, slope, False)
    places = jnp.arange(count)

    def named(tallies, turn):
        used = int((tallies > 0).sum())
        fixed = max(1, used // 4)
        passed = fixed + (places - fixed + turn * (used - fixed)) % max(1, count - fixed)
        return jnp.zeros((count,), jnp.int32).at[order[jnp.where(places < fixed, places, passed)]].set(jnp.asarray(tallies, jnp.int32))

    tallies = jnp.where(number % 4 == 0, named(crowded, number // 4), named(usual, number - number // 4 - 1))
    mixed = jax.random.permutation(jax.random.fold_in(own, 3), count)
    source_of, receiver = mixed[0:count // 2 * 2:2], mixed[1:count // 2 * 2:2]
    slack = jnp.minimum(tallies[source_of] - 1, most - tallies[receiver]) // 2
    slack = jnp.where((source_of == order[0]) | (receiver == order[0]) | (tallies[receiver] == 0), 0, jnp.maximum(slack, 0))
    passed = jax.random.randint(jax.random.fold_in(own, 4), (count // 2,), 0, 1 << 20) % (slack + 1)
    tallies = tallies.at[source_of].add(-passed).at[receiver].add(passed)
    members = jnp.searchsorted(jnp.cumsum(tallies), jnp.arange(rows * top), side="right").astype(jnp.int32)
    grid = members.reshape(top, rows).T
    grid = grid[jax.random.permutation(jax.random.fold_in(own, 1), rows)]
    turn = jax.random.randint(jax.random.fold_in(own, 2), (rows, 1), 0, top)
    return jnp.take_along_axis(grid, (jnp.arange(top)[None, :] + turn) % top, axis=1)


def shares(number_of, total, limit, slope, full):
    portions = [(1 << 20) // math.isqrt(grade ** slope) + 1 for grade in range(1, number_of + 1)]
    largest = limit if full else min(limit, max(-(-total // number_of), total * portions[0] // sum(portions)))
    least = 1 if total - largest >= number_of - 1 else 0
    holding, rest = [largest] + [least] * (number_of - 1), total - largest - least * (number_of - 1)
    while rest > 0:
        candidates = [i for i in range(1, number_of) if holding[i] < largest] or [i for i in range(1, number_of) if holding[i] < limit]
        pool, remaining = sum([portions[i] for i in candidates]), rest
        for i in candidates:
            extra = min(limit - holding[i], max(1, remaining * portions[i] // pool), rest)
            holding[i] = holding[i] + extra
            rest = rest - extra
    return np.array(holding)


def setup_inputs(seed: int = 0) -> dict:
    seeds = jax.random.split(jax.random.key(seed), 4)
    points = draw_points(jax.random.fold_in(seeds[3], 71), 0)
    cluster_of_keys = jax.random.split(jax.random.fold_in(seeds[1], 1), POINTS // P_DEV)
    cluster_of_turns = jax.random.permutation(jax.random.fold_in(seeds[1], 3), POINTS // P_DEV)
    cluster_of = jax.vmap(lambda own, number: assign_block(jax.random.fold_in(seeds[1], 2), own, number, P_DEV, CLUSTERS, 1, MOST, 2))(cluster_of_keys, cluster_of_turns).reshape((POINTS, 1))
    sub_init = with_ends(jax.random.randint(seeds[2], (POINTS,), 0, SUB), jax.random.fold_in(seeds[2], 1), 0, SUB - 1).astype(jnp.int32)
    return {"points": points, "cluster_of": cluster_of, "sub_init": sub_init}


rows_per_piece = 512
softness_level = 8.0


def reference(points, cluster_of, sub_init):
    label = cluster_of[:, 0].astype(jnp.int32)
    order = jnp.argsort(label, stable=True).astype(jnp.int32)
    ordered = jnp.concatenate([points[order], jnp.zeros((rows_per_piece, D), jnp.bfloat16)], axis=0)
    marks = jnp.concatenate([sub_init[order].astype(jnp.int32), jnp.zeros((rows_per_piece,), jnp.int32)], axis=0)
    counts = jnp.sum((label[:, None] == jnp.arange(CLUSTERS, dtype=jnp.int32)[None, :]).astype(jnp.int32), axis=0)
    starts = (jnp.cumsum(counts) - counts).astype(jnp.int32)

    def sweep(current, first):
        def one(cluster):
            start = starts[cluster]
            count = counts[cluster]
            center = current[cluster]
            center16 = center.astype(jnp.bfloat16)
            squared_norm_values = jnp.sum(center * center, axis=1)

            def step(turn, carry):
                sums, mass = carry
                row_position = (turn * rows_per_piece).astype(jnp.int32)
                rows = lax.dynamic_slice_in_dim(ordered, (start + row_position).astype(jnp.int32), rows_per_piece, 0)
                picks = lax.dynamic_slice_in_dim(marks, (start + row_position).astype(jnp.int32), rows_per_piece, 0)
                live = ((row_position + jnp.arange(rows_per_piece, dtype=jnp.int32)) < count).astype(jnp.float32)
                if first:
                    weights = (picks[:, None] == jnp.arange(SUB, dtype=jnp.int32)[None, :]).astype(jnp.float32)
                else:
                    center_products = jnp.dot(rows, center16.T, preferred_element_type=jnp.float32)
                    distance_score = (2.0 * center_products - squared_norm_values[None, :]) / softness_level
                    weights = jax.nn.softmax(distance_score, axis=1)
                weights = (weights * live[:, None]).astype(jnp.bfloat16)
                sums = sums + jnp.dot(weights.T, rows, preferred_element_type=jnp.float32)
                mass = mass + jnp.sum(weights.astype(jnp.float32), axis=0)
                return sums, mass

            tiles = ((count + rows_per_piece - 1) // rows_per_piece).astype(jnp.int32)
            sums, mass = lax.fori_loop(jnp.int32(0), tiles, step,
                                       (jnp.zeros((SUB, D), jnp.float32), jnp.zeros((SUB,), jnp.float32)))
            return sums / (mass[:, None] + 1.0)

        return lax.map(one, jnp.arange(CLUSTERS, dtype=jnp.int32))

    current = sweep(jnp.zeros((CLUSTERS, SUB, D), jnp.float32), True)
    for turn in range(ITERS):
        current = sweep(current, False)
    return jnp.transpose(current, (1, 0, 2))
```

```python
import jax
import jax.numpy as jnp
from jax import lax
from jax.experimental import pallas as pl
from jax.experimental.pallas import tpu as pltpu
from jax.sharding import PartitionSpec as P

SUB = 64
ITERS = 3
CL_DEV = 4
CLUSTERS = 64
MOST = 80
GROUP = 4
WINDOW = 6

MESH = pl.DeviceIdType.MESH
NT = (((1,), (1,)), ((), ()))
f32, bf16, i32 = jnp.float32, jnp.bfloat16, jnp.int32


def link_loads(offset):
    loads = [0.0] * 6
    for axis, step in enumerate(offset):
        loads[2 * axis] += (step == 1) + (step == 2)
        loads[2 * axis + 1] += (step == 3) + (step == 2)
    return loads


def balanced_order():
    left = [(i // 16, i // 4 % 4, i % 4) for i in range(1, 64)]
    state = 12345
    shuffled = []
    while left:
        state = (state * 1103515245 + 12345) % 2**31
        shuffled.append(left.pop((state >> 8) % len(left)))
    left, loads, order = shuffled, [0.0] * 6, []
    while left:
        def unevenness(offset):
            after = [a + b for a, b in zip(loads, link_loads(offset))]
            return max(after) - sum(after) / 6
        best = min(left, key=unevenness)
        left.remove(best)
        order.append(best)
        loads = [a + b for a, b in zip(loads, link_loads(best))]
    return order + [(0, 0, 0)]


ORDER = balanced_order()


def kernel(x_hbm, label_ref, init_ref, out_ref,
           x, packed, block, pick, key, owner, tags, tags_in, live, weights,
           part, part_in, total, final,
           x_sem, own_sem, send, recv, tag_send, tag_recv, part_send, part_recv,
           fin_send, fin_recv, half_send, half_recv, out_sem):
    own, hlp = lax.axis_index("own"), lax.axis_index("help")
    cx, cz, cy, core = own // 4, own % 4, hlp // 2, hlp % 2
    sign = 1 + 2 * core

    def chip(dx, dy, dz):
        return (cx + dx * sign) % 4, (cy + dy * sign) % 4, (cz + dz * sign) % 4

    def device(px, py, pz):
        return (px * 4 + pz, py * 2 + core)

    sibling = (own, cy * 2 + 1 - core)

    barrier = pltpu.get_barrier_semaphore()

    @pl.loop(1, 64)
    def _(i):
        pl.semaphore_signal(barrier, inc=1, device_id=device(*chip(i // 16, i // 4 % 4, i % 4)),
                            device_id_type=MESH)
    pl.semaphore_signal(barrier, inc=1, device_id=sibling, device_id_type=MESH)

    load = pltpu.make_async_copy(x_hbm, x, x_sem)
    load.start()

    slot_id = lax.broadcasted_iota(i32, (CLUSTERS, 1), 0)
    owners = jnp.zeros((CLUSTERS, 1), i32)
    for i, offset in enumerate(ORDER):
        px, py, pz = chip(*offset)
        cluster = px * 16 + pz * 4 + py
        owner[i] = cluster
        owners = jnp.where(slot_id == i, cluster, owners)

    rows = lax.broadcasted_iota(i32, (256, 256), 0)
    cols = lax.broadcasted_iota(i32, (256, 256), 1)
    before = (rows < cols).astype(f32).astype(bf16)
    counts = jnp.zeros((CLUSTERS, 1), f32)
    tag = jnp.zeros((CLUSTERS, 128), f32)
    for j in range(16):
        label = label_ref[:, pl.ds(j * 256, 256)]
        member = (label == owners).astype(f32)
        earlier = jnp.dot(member.astype(bf16), before, preferred_element_type=f32) + counts
        counts = counts + jnp.sum(member, axis=1, keepdims=True)
        rank = jnp.sum(member * earlier, axis=0, keepdims=True).astype(i32)
        key[:, pl.ds(j * 256, 256)] = label * 128 + rank
        at_rank = (rank == lax.broadcasted_iota(i32, (128, 256), 0)).astype(f32).astype(bf16)
        mark = (member * (init_ref[:, pl.ds(j * 256, 256)] + 1).astype(f32)).astype(bf16)
        tag = tag + lax.dot_general(mark, at_rank, NT, preferred_element_type=f32)
    for i in range(CLUSTERS):
        tags[i] = jnp.broadcast_to(tag[i:i + 1, :], (8, 128))
    tags_in[CLUSTERS - 1] = jnp.broadcast_to(tag[CLUSTERS - 1:, :], (8, 128))

    load.wait()
    pl.semaphore_wait(barrier, 64)

    def rows_copy(i, target):
        return pltpu.make_async_remote_copy(
            src_ref=packed.at[i], dst_ref=block.at[i], send_sem=send.at[i], recv_sem=recv.at[i],
            device_id=target, device_id_type=MESH)

    def tags_copy(i, target):
        return pltpu.make_async_remote_copy(
            src_ref=tags.at[i], dst_ref=tags_in.at[i], send_sem=tag_send.at[i], recv_sem=tag_recv.at[i],
            device_id=target, device_id_type=MESH)

    @pl.loop(0, CLUSTERS // GROUP)
    def _(g):
        where = key[...]
        for j in range(GROUP):
            shifted = where - owner[g * GROUP + j] * 128
            pick[pl.ds(j * MOST, MOST), :] = (
                shifted == lax.broadcasted_iota(i32, (MOST, 1), 0)).astype(f32).astype(bf16)
        for n in range(4):
            moved = jnp.dot(pick[...], x[:, n * 256:(n + 1) * 256], preferred_element_type=f32)
            packed[pl.ds(g * GROUP, GROUP), :, n * 256:(n + 1) * 256] = (
                moved.astype(bf16).reshape(GROUP, MOST, 256))
        for j in range(GROUP):
            i = g * GROUP + j
            code = jnp.int32(0)
            for k in range(CLUSTERS // GROUP):
                ox, oy, oz = ORDER[k * GROUP + j]
                code = jnp.where(g == k, ox * 16 + oy * 4 + oz, code)
            target = device(*chip(code // 16, code // 4 % 4, code % 4))

            @pl.when(i >= WINDOW)
            def _():
                rows_copy(i - WINDOW, sibling).wait_send()
                tags_copy(i - WINDOW, sibling).wait_send()

            @pl.when(i < CLUSTERS - 1)
            def _():
                tags_copy(i, target).start()
                rows_copy(i, target).start()

    keep = pltpu.make_async_copy(packed.at[CLUSTERS - 1], block.at[CLUSTERS - 1], own_sem)
    keep.start()
    keep.wait()

    lane = lax.broadcasted_iota(i32, (128, 8 * MOST), 1)
    row = lax.broadcasted_iota(i32, (128, 8 * MOST), 0)
    spread = jnp.zeros((128, 8 * MOST), f32)
    for j in range(8):
        spread = jnp.where(lane - row == j * MOST, 1.0, spread)
    spread = jnp.where(row < MOST, spread, 0.0).astype(bf16)
    lane8 = lax.broadcasted_iota(i32, (8, 8 * MOST), 1) - MOST * lax.broadcasted_iota(i32, (8, 8 * MOST), 0)
    in_block = ((lane8 >= 0) & (lane8 < MOST)).astype(f32)
    total[...] = jnp.zeros_like(total)

    @pl.loop(0, 8)
    def _(g):
        for j in range(8):
            i = g * 8 + j

            @pl.when(i < CLUSTERS - 1)
            def _():
                tags_copy(i, sibling).wait_recv()
                rows_copy(i, sibling).wait_recv()
        marks = tags_in[pl.ds(g * 8, 8), 0, :].astype(bf16)
        mark = jnp.sum(jnp.dot(marks, spread, preferred_element_type=f32) * in_block,
                       axis=0, keepdims=True)
        start = pl.multiple_of(g * 8 * MOST, 128)
        live[0:1, pl.ds(start, 8 * MOST)] = (mark > 0.0).astype(f32)
        chosen = (mark.astype(i32) == lax.broadcasted_iota(i32, (SUB, 1), 0) + 1).astype(f32)
        data = block[pl.ds(g * 8, 8)].reshape(8 * MOST, 1024)
        total[:, :1024] += jnp.dot(chosen.astype(bf16), data, preferred_element_type=f32)
        total[:, 1024:] += sum(chosen[:, k * 128:(k + 1) * 128] for k in range(5))

    part[0, :, :1024] = total[:, :1024]
    part[0, :, 1024:] = jnp.broadcast_to(jnp.sum(total[:, 1024:], axis=1, keepdims=True), (SUB, 128))

    for k in range(WINDOW - 1):
        rows_copy(CLUSTERS - 1 - WINDOW + 1 + k, sibling).wait_send()
        tags_copy(CLUSTERS - 1 - WINDOW + 1 + k, sibling).wait_send()

    def combine(t):
        swap = pltpu.make_async_remote_copy(
            src_ref=part.at[t], dst_ref=part_in.at[t], send_sem=part_send.at[t], recv_sem=part_recv.at[t],
            device_id=sibling, device_id_type=MESH)
        swap.start()
        swap.wait()
        mass = part[t, :, 1024:1025] + part_in[t, :, 1024:1025]
        return (part[t, :, :1024] + part_in[t, :, :1024]) / (mass + 1.0)

    @pl.loop(0, ITERS)
    def _(t):
        current = combine(t)
        current16 = current.astype(bf16)
        squared = jnp.sum(current * current, axis=1, keepdims=True) * 0.125
        mass = jnp.zeros((SUB, 128), f32)
        for g in range(8):
            data = block[g * 8:(g + 1) * 8].reshape(8 * MOST, 1024)
            product = lax.dot_general(current16, data, NT, preferred_element_type=f32)
            score = product * 0.25 - squared
            grown = jnp.exp(score - jnp.max(score, axis=0, keepdims=True))
            alive = live[0:1, g * 8 * MOST:(g + 1) * 8 * MOST]
            weight = (grown / jnp.sum(grown, axis=0, keepdims=True) * alive).astype(bf16)
            weights[:, g * 8 * MOST:(g + 1) * 8 * MOST] = weight
            wide = weight.astype(f32)
            mass = mass + sum(wide[:, k * 128:(k + 1) * 128] for k in range(5))
        part[t + 1, :, 1024:] = jnp.broadcast_to(jnp.sum(mass, axis=1, keepdims=True), (SUB, 128))
        for n in range(4):
            data = block[:, :, n * 256:(n + 1) * 256].reshape(CLUSTERS * MOST, 256)
            part[t + 1, :, n * 256:(n + 1) * 256] = jnp.dot(
                weights[...], data, preferred_element_type=f32)

    final[cy] = combine(ITERS)

    half = pl.ds(core * 32, 32)

    def along(d):
        return pltpu.make_async_remote_copy(
            src_ref=final.at[cy, half], dst_ref=final.at[cy, half],
            send_sem=fin_send.at[d], recv_sem=fin_recv.at[d],
            device_id=(own, (cy + d) % 4 * 2 + core), device_id_type=MESH)

    def across(d):
        there = final.at[(cy + 4 - d) % 4, half]
        return pltpu.make_async_remote_copy(
            src_ref=there, dst_ref=there, send_sem=half_send.at[d], recv_sem=half_recv.at[d],
            device_id=sibling, device_id_type=MESH)

    for d in (1, 3, 2):
        along(d).start()
    for d in (1, 3, 2):
        along(d).wait_recv()
        across(d).start()
    for d in (1, 3, 2):
        along(d).wait_send()
        across(d).wait()
    store = pltpu.make_async_copy(final, out_ref, out_sem)
    store.start()
    store.wait()


def shards(points, cluster_of, sub_init):
    rows, width = points.shape
    dma = pltpu.SemaphoreType.DMA
    result = pl.pallas_call(
        kernel,
        out_shape=jax.ShapeDtypeStruct((CL_DEV, SUB, width), f32),
        in_specs=[pl.BlockSpec(memory_space=pl.ANY)] + [pl.BlockSpec(memory_space=pltpu.VMEM)] * 2,
        out_specs=pl.BlockSpec(memory_space=pl.ANY),
        scratch_shapes=[
            pltpu.VMEM((rows, width), bf16),
            pltpu.VMEM((CLUSTERS, MOST, width), bf16),
            pltpu.VMEM((CLUSTERS, MOST, width), bf16),
            pltpu.VMEM((GROUP * MOST, rows), bf16),
            pltpu.VMEM((1, rows), i32),
            pltpu.SMEM((CLUSTERS,), i32),
            pltpu.VMEM((CLUSTERS, 8, 128), f32),
            pltpu.VMEM((CLUSTERS, 8, 128), f32),
            pltpu.VMEM((8, CLUSTERS * MOST), f32),
            pltpu.VMEM((SUB, CLUSTERS * MOST), bf16),
            pltpu.VMEM((ITERS + 1, SUB, width + 128), f32),
            pltpu.VMEM((ITERS + 1, SUB, width + 128), f32),
            pltpu.VMEM((SUB, width + 128), f32),
            pltpu.VMEM((CL_DEV, SUB, width), f32),
            dma, dma, dma((CLUSTERS,)), dma((CLUSTERS,)), dma((CLUSTERS,)), dma((CLUSTERS,)),
            dma((ITERS + 1,)), dma((ITERS + 1,)),
            dma((4,)), dma((4,)), dma((4,)), dma((4,)), dma,
        ],
        compiler_params=pltpu.CompilerParams(
            collective_id=0, has_side_effects=True, vmem_limit_bytes=56 * 2**20),
    )(points, cluster_of.reshape(1, rows), sub_init.reshape(1, rows))
    return jnp.transpose(result, (1, 0, 2))


def solution(mesh):
    in_specs = (P(("own", "help"), None), P(("own", "help"), None), P(("own", "help")))
    out_specs = P(None, "own", None)
    return jax.shard_map(shards, mesh=mesh, in_specs=in_specs, out_specs=out_specs, check_vma=False)
```

```python
import jax
import jax.numpy as jnp
from jax import lax
from jax.experimental import pallas as pl
from jax.experimental.pallas import tpu as pltpu
from jax.sharding import PartitionSpec as P

SUB = 64
ITERS = 3
CL_DEV = 4
CLUSTERS = 64
MOST = 80
GROUP = 4
WINDOW = 6

MESH = pl.DeviceIdType.MESH
NT = (((1,), (1,)), ((), ()))
f32, bf16, i32 = jnp.float32, jnp.bfloat16, jnp.int32


CODES = [
    42, 58, 16, 41, 3, 43, 1, 46, 4, 38, 12, 26, 48, 54, 28, 34, 8, 59, 17, 45, 7, 30, 52, 47, 5,
    62, 20, 37, 15, 22, 60, 10, 32, 39, 13, 40, 2, 27, 49, 57, 19, 25, 51, 61, 23, 6, 44, 50, 24,
    29, 55, 18, 56, 63, 21, 11, 33, 36, 14, 53, 31, 35, 9, 0,
]
ORDER = [(code // 16, code // 4 % 4, code % 4) for code in CODES]


def kernel(x_hbm, label_ref, init_ref, out_ref,
           x, packed, block, pick, key, owner, tags, tags_in, live, weights,
           part, part_in, total, final,
           x_sem, own_sem, send, recv, tag_send, tag_recv, part_send, part_recv,
           fin_send, fin_recv, half_send, half_recv, out_sem):
    own, hlp = lax.axis_index("own"), lax.axis_index("help")
    cx, cz, cy, core = own // 4, own % 4, hlp // 2, hlp % 2
    sign = 1 + 2 * core

    def chip(dx, dy, dz):
        return (cx + dx * sign) % 4, (cy + dy * sign) % 4, (cz + dz * sign) % 4

    def device(px, py, pz):
        return (px * 4 + pz, py * 2 + core)

    sibling = (own, cy * 2 + 1 - core)

    barrier = pltpu.get_barrier_semaphore()

    @pl.loop(1, 64)
    def _(i):
        pl.semaphore_signal(barrier, inc=1, device_id=device(*chip(i // 16, i // 4 % 4, i % 4)),
                            device_id_type=MESH)
    pl.semaphore_signal(barrier, inc=1, device_id=sibling, device_id_type=MESH)

    load = pltpu.make_async_copy(x_hbm, x, x_sem)
    load.start()

    slot_id = lax.broadcasted_iota(i32, (CLUSTERS, 1), 0)
    owners = jnp.zeros((CLUSTERS, 1), i32)
    for i, offset in enumerate(ORDER):
        px, py, pz = chip(*offset)
        cluster = px * 16 + pz * 4 + py
        owner[i] = cluster
        owners = jnp.where(slot_id == i, cluster, owners)

    rows = lax.broadcasted_iota(i32, (256, 256), 0)
    cols = lax.broadcasted_iota(i32, (256, 256), 1)
    before = (rows < cols).astype(f32).astype(bf16)
    counts = jnp.zeros((CLUSTERS, 1), f32)
    tag = jnp.zeros((CLUSTERS, 128), f32)
    for j in range(16):
        label = label_ref[:, pl.ds(j * 256, 256)]
        member = (label == owners).astype(f32)
        earlier = jnp.dot(member.astype(bf16), before, preferred_element_type=f32) + counts
        counts = counts + jnp.sum(member, axis=1, keepdims=True)
        rank = jnp.sum(member * earlier, axis=0, keepdims=True).astype(i32)
        key[:, pl.ds(j * 256, 256)] = label * 128 + rank
        at_rank = (rank == lax.broadcasted_iota(i32, (128, 256), 0)).astype(f32).astype(bf16)
        mark = (member * (init_ref[:, pl.ds(j * 256, 256)] + 1).astype(f32)).astype(bf16)
        tag = tag + lax.dot_general(mark, at_rank, NT, preferred_element_type=f32)
    for i in range(CLUSTERS):
        tags[i] = jnp.broadcast_to(tag[i:i + 1, :], (8, 128))
    tags_in[CLUSTERS - 1] = jnp.broadcast_to(tag[CLUSTERS - 1:, :], (8, 128))

    load.wait()

    def slots(i):
        return pl.ds(pl.multiple_of(i * MOST, 16), MOST)

    def rows_copy(i, target):
        return pltpu.make_async_remote_copy(
            src_ref=packed.at[slots(i)], dst_ref=block.at[slots(i)],
            send_sem=send, recv_sem=recv.at[i],
            device_id=target, device_id_type=MESH)

    def tags_copy(i, target):
        return pltpu.make_async_remote_copy(
            src_ref=tags.at[i], dst_ref=tags_in.at[i], send_sem=tag_send.at[i], recv_sem=tag_recv.at[i],
            device_id=target, device_id_type=MESH)

    groups = CLUSTERS // GROUP

    @pl.loop(0, groups + 1)
    def _(g):
        @pl.when(g < groups)
        def _():
            where = key[...]
            for j in range(GROUP):
                shifted = where - owner[g * GROUP + j] * 128
                pick[pl.ds(j * MOST, MOST), :] = (
                    shifted == lax.broadcasted_iota(i32, (MOST, 1), 0)).astype(f32).astype(bf16)

        @pl.when(g == 1)
        def _():
            pl.semaphore_wait(barrier, 64)

        for n in range(GROUP):
            @pl.when(g < groups)
            def _():
                moved = jnp.dot(pick[...], x[:, n * 256:(n + 1) * 256], preferred_element_type=f32)
                start = pl.multiple_of(g * GROUP * MOST, 16)
                packed[pl.ds(start, GROUP * MOST), n * 256:(n + 1) * 256] = moved.astype(bf16)

            i = (g - 1) * GROUP + n
            code = jnp.int32(0)
            for k in range(groups):
                ox, oy, oz = ORDER[k * GROUP + n]
                code = jnp.where(g == k + 1, ox * 16 + oy * 4 + oz, code)
            target = device(*chip(code // 16, code // 4 % 4, code % 4))

            @pl.when(i >= WINDOW)
            def _():
                rows_copy(0, sibling).wait_send()

            @pl.when((i >= 0) & (i < CLUSTERS - 1))
            def _():
                tags_copy(i, target).start()
                rows_copy(i, target).start()

    keep = pltpu.make_async_copy(
        packed.at[slots(CLUSTERS - 1)], block.at[slots(CLUSTERS - 1)], own_sem)
    keep.start()
    keep.wait()

    lane = lax.broadcasted_iota(i32, (128, 8 * MOST), 1)
    row = lax.broadcasted_iota(i32, (128, 8 * MOST), 0)
    spread = jnp.zeros((128, 8 * MOST), f32)
    for j in range(8):
        spread = jnp.where(lane - row == j * MOST, 1.0, spread)
    spread = jnp.where(row < MOST, spread, 0.0).astype(bf16)
    lane8 = lax.broadcasted_iota(i32, (8, 8 * MOST), 1) - MOST * lax.broadcasted_iota(i32, (8, 8 * MOST), 0)
    in_block = ((lane8 >= 0) & (lane8 < MOST)).astype(f32)
    total[...] = jnp.zeros_like(total)

    @pl.loop(0, 8)
    def _(g):
        for j in range(8):
            i = g * 8 + j

            @pl.when(i < CLUSTERS - 1)
            def _():
                tags_copy(i, sibling).wait_recv()
                rows_copy(i, sibling).wait_recv()
        marks = tags_in[pl.ds(g * 8, 8), 0, :].astype(bf16)
        mark = jnp.sum(jnp.dot(marks, spread, preferred_element_type=f32) * in_block,
                       axis=0, keepdims=True)
        start = pl.multiple_of(g * 8 * MOST, 128)
        live[0:1, pl.ds(start, 8 * MOST)] = (mark > 0.0).astype(f32)
        chosen = (mark.astype(i32) == lax.broadcasted_iota(i32, (SUB, 1), 0) + 1).astype(f32)
        data = block[pl.ds(start, 8 * MOST), :]
        total[:, :1024] += jnp.dot(chosen.astype(bf16), data, preferred_element_type=f32)
        total[:, 1024:] += sum(chosen[:, k * 128:(k + 1) * 128] for k in range(5))

    part[0, :, :1024] = total[:, :1024]
    part[0, :, 1024:] = jnp.broadcast_to(jnp.sum(total[:, 1024:], axis=1, keepdims=True), (SUB, 128))

    @pl.loop(0, WINDOW - 1)
    def _(k):
        rows_copy(0, sibling).wait_send()

    @pl.loop(0, CLUSTERS - 1)
    def _(i):
        tags_copy(i, sibling).wait_send()

    def combine(t):
        swap = pltpu.make_async_remote_copy(
            src_ref=part.at[t], dst_ref=part_in.at[t], send_sem=part_send.at[t], recv_sem=part_recv.at[t],
            device_id=sibling, device_id_type=MESH)
        swap.start()
        swap.wait()
        mass = part[t, :, 1024:1025] + part_in[t, :, 1024:1025]
        return (part[t, :, :1024] + part_in[t, :, :1024]) / (mass + 1.0)

    @pl.loop(0, ITERS)
    def _(t):
        current = combine(t)
        current16 = current.astype(bf16)
        squared = jnp.sum(current * current, axis=1, keepdims=True) * 0.125
        mass = jnp.zeros((SUB, 128), f32)
        for g in range(8):
            data = block[g * 8 * MOST:(g + 1) * 8 * MOST, :]
            product = lax.dot_general(current16, data, NT, preferred_element_type=f32)
            score = product * 0.25 - squared
            grown = jnp.exp(score - jnp.max(score, axis=0, keepdims=True))
            alive = live[0:1, g * 8 * MOST:(g + 1) * 8 * MOST]
            weight = (grown / jnp.sum(grown, axis=0, keepdims=True) * alive).astype(bf16)
            weights[:, g * 8 * MOST:(g + 1) * 8 * MOST] = weight
            wide = weight.astype(f32)
            mass = mass + sum(wide[:, k * 128:(k + 1) * 128] for k in range(5))
        part[t + 1, :, 1024:] = jnp.broadcast_to(jnp.sum(mass, axis=1, keepdims=True), (SUB, 128))
        for n in range(4):
            data = block[:, n * 256:(n + 1) * 256]
            part[t + 1, :, n * 256:(n + 1) * 256] = jnp.dot(
                weights[...], data, preferred_element_type=f32)

    final[cy] = combine(ITERS)

    half = pl.ds(core * 32, 32)

    def along(d):
        return pltpu.make_async_remote_copy(
            src_ref=final.at[cy, half], dst_ref=final.at[cy, half],
            send_sem=fin_send.at[d], recv_sem=fin_recv.at[d],
            device_id=(own, (cy + d) % 4 * 2 + core), device_id_type=MESH)

    def across(d):
        there = final.at[(cy + 4 - d) % 4, half]
        return pltpu.make_async_remote_copy(
            src_ref=there, dst_ref=there, send_sem=half_send.at[d], recv_sem=half_recv.at[d],
            device_id=sibling, device_id_type=MESH)

    for d in (1, 3, 2):
        along(d).start()
    for d in (1, 3, 2):
        along(d).wait_recv()
        across(d).start()
    for d in (1, 3, 2):
        along(d).wait_send()
        across(d).wait()
    store = pltpu.make_async_copy(final, out_ref, out_sem)
    store.start()
    store.wait()


def shards(points, cluster_of, sub_init):
    rows, width = points.shape
    dma = pltpu.SemaphoreType.DMA
    result = pl.pallas_call(
        kernel,
        out_shape=jax.ShapeDtypeStruct((CL_DEV, SUB, width), f32),
        in_specs=[pl.BlockSpec(memory_space=pl.ANY)] + [pl.BlockSpec(memory_space=pltpu.VMEM)] * 2,
        out_specs=pl.BlockSpec(memory_space=pl.ANY),
        scratch_shapes=[
            pltpu.VMEM((rows, width), bf16),
            pltpu.VMEM((CLUSTERS * MOST, width), bf16),
            pltpu.VMEM((CLUSTERS * MOST, width), bf16),
            pltpu.VMEM((GROUP * MOST, rows), bf16),
            pltpu.VMEM((1, rows), i32),
            pltpu.SMEM((CLUSTERS,), i32),
            pltpu.VMEM((CLUSTERS, 8, 128), f32),
            pltpu.VMEM((CLUSTERS, 8, 128), f32),
            pltpu.VMEM((8, CLUSTERS * MOST), f32),
            pltpu.VMEM((SUB, CLUSTERS * MOST), bf16),
            pltpu.VMEM((ITERS + 1, SUB, width + 128), f32),
            pltpu.VMEM((ITERS + 1, SUB, width + 128), f32),
            pltpu.VMEM((SUB, width + 128), f32),
            pltpu.VMEM((CL_DEV, SUB, width), f32),
            dma, dma, dma, dma((CLUSTERS,)), dma((CLUSTERS,)), dma((CLUSTERS,)),
            dma((ITERS + 1,)), dma((ITERS + 1,)),
            dma((4,)), dma((4,)), dma((4,)), dma((4,)), dma,
        ],
        compiler_params=pltpu.CompilerParams(
            collective_id=0, has_side_effects=True, vmem_limit_bytes=56 * 2**20),
    )(points, cluster_of.reshape(1, rows), sub_init.reshape(1, rows))
    return jnp.transpose(result, (1, 0, 2))


def solution(mesh):
    in_specs = (P(("own", "help"), None), P(("own", "help"), None), P(("own", "help")))
    out_specs = P(None, "own", None)
    return jax.shard_map(shards, mesh=mesh, in_specs=in_specs, out_specs=out_specs, check_vma=False)
```

```python
import jax
import jax.numpy as jnp
from jax import lax
from jax.experimental import pallas as pl
from jax.experimental.pallas import tpu as pltpu
from jax.sharding import PartitionSpec as P

SUB = 64
ITERS = 3
CL_DEV = 4
CLUSTERS = 64
MOST = 80
GROUP = 4
WINDOW = 6
QUARTERS = 4

MESH = pl.DeviceIdType.MESH
NT = (((1,), (1,)), ((), ()))
f32, bf16, i32 = jnp.float32, jnp.bfloat16, jnp.int32


CODES = [
    42, 58, 16, 41, 3, 43, 1, 46, 4, 38, 12, 26, 48, 54, 28, 34, 8, 59, 17, 45, 7, 30, 52, 47, 5,
    62, 20, 37, 15, 22, 60, 10, 32, 39, 13, 40, 2, 27, 49, 57, 19, 25, 51, 61, 23, 6, 44, 50, 24,
    29, 55, 18, 56, 63, 21, 11, 33, 36, 14, 53, 31, 35, 9, 0,
]
ORDER = [(code // 16, code // 4 % 4, code % 4) for code in CODES]


def kernel(x_hbm, label_ref, init_ref, out_ref,
           x, packed, block, turned, pick, key, owner, tags, tags_in, live, weights,
           part, part_in, mass, mass_in, centre, final,
           x_sem, own_sem, send, recv, tag_send, tag_recv, part_send, part_recv,
           fin_send, fin_recv, half_send, half_recv, out_sem):
    own, hlp = lax.axis_index("own"), lax.axis_index("help")
    cx, cz, cy, core = own // 4, own % 4, hlp // 2, hlp % 2
    sign = 1 + 2 * core

    def chip(dx, dy, dz):
        return (cx + dx * sign) % 4, (cy + dy * sign) % 4, (cz + dz * sign) % 4

    def device(px, py, pz):
        return (px * 4 + pz, py * 2 + core)

    sibling = (own, cy * 2 + 1 - core)

    barrier = pltpu.get_barrier_semaphore()

    @pl.loop(1, 64)
    def _(i):
        pl.semaphore_signal(barrier, inc=1, device_id=device(*chip(i // 16, i // 4 % 4, i % 4)),
                            device_id_type=MESH)
    pl.semaphore_signal(barrier, inc=1, device_id=sibling, device_id_type=MESH)

    load = pltpu.make_async_copy(x_hbm, x, x_sem)
    load.start()

    slot_id = lax.broadcasted_iota(i32, (CLUSTERS, 1), 0)
    owners = jnp.zeros((CLUSTERS, 1), i32)
    for i, offset in enumerate(ORDER):
        px, py, pz = chip(*offset)
        cluster = px * 16 + pz * 4 + py
        owner[i] = cluster
        owners = jnp.where(slot_id == i, cluster, owners)

    rows = lax.broadcasted_iota(i32, (256, 256), 0)
    cols = lax.broadcasted_iota(i32, (256, 256), 1)
    before = (rows < cols).astype(f32).astype(bf16)
    counts = jnp.zeros((CLUSTERS, 1), f32)
    tag = jnp.zeros((CLUSTERS, 128), f32)
    for j in range(16):
        label = label_ref[:, pl.ds(j * 256, 256)]
        member = (label == owners).astype(f32)
        earlier = jnp.dot(member.astype(bf16), before, preferred_element_type=f32) + counts
        counts = counts + jnp.sum(member, axis=1, keepdims=True)
        rank = jnp.sum(member * earlier, axis=0, keepdims=True).astype(i32)
        key[:, pl.ds(j * 256, 256)] = label * 128 + rank
        at_rank = (rank == lax.broadcasted_iota(i32, (128, 256), 0)).astype(f32).astype(bf16)
        mark = (member * (init_ref[:, pl.ds(j * 256, 256)] + 1).astype(f32)).astype(bf16)
        tag = tag + lax.dot_general(mark, at_rank, NT, preferred_element_type=f32)
    for i in range(CLUSTERS):
        tags[i] = jnp.broadcast_to(tag[i:i + 1, :], (8, 128))
    tags_in[CLUSTERS - 1] = jnp.broadcast_to(tag[CLUSTERS - 1:, :], (8, 128))

    load.wait()

    def slots(i):
        return pl.ds(pl.multiple_of(i * MOST, 16), MOST)

    def rows_copy(i, target):
        return pltpu.make_async_remote_copy(
            src_ref=packed.at[slots(i)], dst_ref=block.at[slots(i)],
            send_sem=send, recv_sem=recv.at[i],
            device_id=target, device_id_type=MESH)

    def tags_copy(i, target):
        return pltpu.make_async_remote_copy(
            src_ref=tags.at[i], dst_ref=tags_in.at[i], send_sem=tag_send.at[i], recv_sem=tag_recv.at[i],
            device_id=target, device_id_type=MESH)

    groups = CLUSTERS // GROUP

    @pl.loop(0, groups + 1)
    def _(g):
        @pl.when(g < groups)
        def _():
            where = key[...]
            for j in range(GROUP):
                shifted = where - owner[g * GROUP + j] * 128
                pick[pl.ds(j * MOST, MOST), :] = (
                    shifted == lax.broadcasted_iota(i32, (MOST, 1), 0)).astype(f32).astype(bf16)

        @pl.when(g == 1)
        def _():
            pl.semaphore_wait(barrier, 64)

        for n in range(GROUP):
            @pl.when(g < groups)
            def _():
                moved = jnp.dot(pick[...], x[:, n * 256:(n + 1) * 256], preferred_element_type=f32)
                start = pl.multiple_of(g * GROUP * MOST, 16)
                packed[pl.ds(start, GROUP * MOST), n * 256:(n + 1) * 256] = moved.astype(bf16)

            i = (g - 1) * GROUP + n
            code = jnp.int32(0)
            for k in range(groups):
                ox, oy, oz = ORDER[k * GROUP + n]
                code = jnp.where(g == k + 1, ox * 16 + oy * 4 + oz, code)
            target = device(*chip(code // 16, code // 4 % 4, code % 4))

            @pl.when(i >= WINDOW)
            def _():
                rows_copy(0, sibling).wait_send()

            @pl.when((i >= 0) & (i < CLUSTERS - 1))
            def _():
                tags_copy(i, target).start()
                rows_copy(i, target).start()

    keep = pltpu.make_async_copy(
        packed.at[slots(CLUSTERS - 1)], block.at[slots(CLUSTERS - 1)], own_sem)
    keep.start()
    keep.wait()

    lane = lax.broadcasted_iota(i32, (128, 8 * MOST), 1)
    row = lax.broadcasted_iota(i32, (128, 8 * MOST), 0)
    spread = jnp.zeros((128, 8 * MOST), f32)
    for j in range(8):
        spread = jnp.where(lane - row == j * MOST, 1.0, spread)
    spread = jnp.where(row < MOST, spread, 0.0).astype(bf16)
    lane8 = lax.broadcasted_iota(i32, (8, 8 * MOST), 1) - MOST * lax.broadcasted_iota(i32, (8, 8 * MOST), 0)
    in_block = ((lane8 >= 0) & (lane8 < MOST)).astype(f32)
    part[0] = jnp.zeros_like(part[0])
    mass[0] = jnp.zeros_like(mass[0])

    @pl.loop(0, 8)
    def _(g):
        for j in range(8):
            i = g * 8 + j

            @pl.when(i < CLUSTERS - 1)
            def _():
                tags_copy(i, sibling).wait_recv()
                rows_copy(i, sibling).wait_recv()
        marks = tags_in[pl.ds(g * 8, 8), 0, :].astype(bf16)
        mark = jnp.sum(jnp.dot(marks, spread, preferred_element_type=f32) * in_block,
                       axis=0, keepdims=True)
        start = pl.multiple_of(g * 8 * MOST, 128)
        live[0:1, pl.ds(start, 8 * MOST)] = (mark > 0.0).astype(f32)
        chosen = (mark.astype(i32) == lax.broadcasted_iota(i32, (SUB, 1), 0) + 1).astype(f32)
        data = block[pl.ds(start, 8 * MOST), :]
        turned[:, pl.ds(start, 8 * MOST)] = data.T
        for n in range(QUARTERS):
            part[0, n] += jnp.dot(chosen.astype(bf16), data[:, n * 256:(n + 1) * 256],
                                  preferred_element_type=f32)
        mass[0] += sum(chosen[:, k * 128:(k + 1) * 128] for k in range(5))

    def swap(t, n):
        return pltpu.make_async_remote_copy(
            src_ref=part.at[t, n], dst_ref=part_in.at[t, n],
            send_sem=part_send.at[t * 5 + n], recv_sem=part_recv.at[t * 5 + n],
            device_id=sibling, device_id_type=MESH)

    def swap_mass(t):
        return pltpu.make_async_remote_copy(
            src_ref=mass.at[t], dst_ref=mass_in.at[t],
            send_sem=part_send.at[t * 5 + 4], recv_sem=part_recv.at[t * 5 + 4],
            device_id=sibling, device_id_type=MESH)

    def divisor(t):
        swap_mass(t).wait_recv()
        return jnp.sum(mass[t] + mass_in[t], axis=1, keepdims=True) + 1.0

    def combine(t, n, below):
        swap(t, n).wait_recv()
        current = (part[t, n] + part_in[t, n]) / below
        final[cy, n] = current
        centre[:, n * 256:(n + 1) * 256] = current.astype(bf16)
        return jnp.sum(current * current, axis=1, keepdims=True)

    half = pl.ds(core * 32, 32)

    def along(d, n):
        return pltpu.make_async_remote_copy(
            src_ref=final.at[cy, n, half], dst_ref=final.at[cy, n, half],
            send_sem=fin_send.at[d * 4 + n], recv_sem=fin_recv.at[d * 4 + n],
            device_id=(own, (cy + d) % 4 * 2 + core), device_id_type=MESH)

    def across(d, n):
        there = final.at[(cy + 4 - d) % 4, n, half]
        return pltpu.make_async_remote_copy(
            src_ref=there, dst_ref=there,
            send_sem=half_send.at[d * 4 + n], recv_sem=half_recv.at[d * 4 + n],
            device_id=sibling, device_id_type=MESH)

    def store(d, n):
        j = (cy + 4 - d) % 4
        return pltpu.make_async_copy(
            final.at[j, n], out_ref.at[j, :, pl.ds(n * 256, 256)], out_sem.at[d * 4 + n])

    swap_mass(0).start()
    for n in range(QUARTERS):
        swap(0, n).start()
    below = divisor(0)
    squared = jnp.zeros((SUB, 1), f32)
    for n in range(QUARTERS):
        squared = squared + combine(0, n, below)

    def iteration(t, squared):
        bias = squared * 0.125
        heavy = jnp.zeros((SUB, 128), f32)
        for g in range(8):
            lanes = slice(g * 8 * MOST, (g + 1) * 8 * MOST)
            product = jnp.dot(centre[...], turned[:, lanes], preferred_element_type=f32)
            score = product * 0.25 - bias
            grown = jnp.exp(score - jnp.max(score, axis=0, keepdims=True))
            weight = (grown / jnp.sum(grown, axis=0, keepdims=True) * live[0:1, lanes]).astype(bf16)
            weights[:, lanes] = weight
            wide = weight.astype(f32)
            heavy = heavy + sum(wide[:, k * 128:(k + 1) * 128] for k in range(5))
        mass[t + 1] = heavy
        swap_mass(t + 1).start()

        def finish(n, below):
            after = combine(t + 1, n, below)

            @pl.when(t == ITERS - 1)
            def _():
                for d in (1, 3, 2):
                    along(d, n).start()
            return after

        squared = jnp.zeros((SUB, 1), f32)
        for n in range(QUARTERS):
            part[t + 1, n] = jnp.dot(weights[...], block[:, n * 256:(n + 1) * 256],
                                     preferred_element_type=f32)
            swap(t + 1, n).start()
            if n == 0:
                below = divisor(t + 1)
            else:
                squared = squared + finish(n - 1, below)
        return squared + finish(QUARTERS - 1, below)

    lax.fori_loop(0, ITERS, iteration, squared)

    for n in range(QUARTERS):
        store(0, n).start()
    for n in range(QUARTERS):
        for d in (1, 3, 2):
            along(d, n).wait_recv()
            across(d, n).start()
    for n in range(QUARTERS):
        for d in (1, 3, 2):
            across(d, n).wait_recv()
            store(d, n).start()

    @pl.loop(0, WINDOW - 1)
    def _(k):
        rows_copy(0, sibling).wait_send()

    @pl.loop(0, CLUSTERS - 1)
    def _(i):
        tags_copy(i, sibling).wait_send()

    for t in range(ITERS + 1):
        swap_mass(t).wait_send()
        for n in range(QUARTERS):
            swap(t, n).wait_send()
    for n in range(QUARTERS):
        store(0, n).wait()
        for d in (1, 3, 2):
            along(d, n).wait_send()
            across(d, n).wait_send()
            store(d, n).wait()


def shards(points, cluster_of, sub_init):
    rows, width = points.shape
    dma = pltpu.SemaphoreType.DMA
    result = pl.pallas_call(
        kernel,
        out_shape=jax.ShapeDtypeStruct((CL_DEV, SUB, width), f32),
        in_specs=[pl.BlockSpec(memory_space=pl.ANY)] + [pl.BlockSpec(memory_space=pltpu.VMEM)] * 2,
        out_specs=pl.BlockSpec(memory_space=pl.ANY),
        scratch_shapes=[
            pltpu.VMEM((rows, width), bf16),
            pltpu.VMEM((CLUSTERS * MOST, width), bf16),
            pltpu.VMEM((CLUSTERS * MOST, width), bf16),
            pltpu.VMEM((width, CLUSTERS * MOST), bf16),
            pltpu.VMEM((GROUP * MOST, rows), bf16),
            pltpu.VMEM((1, rows), i32),
            pltpu.SMEM((CLUSTERS,), i32),
            pltpu.VMEM((CLUSTERS, 8, 128), f32),
            pltpu.VMEM((CLUSTERS, 8, 128), f32),
            pltpu.VMEM((8, CLUSTERS * MOST), f32),
            pltpu.VMEM((SUB, CLUSTERS * MOST), bf16),
            pltpu.VMEM((ITERS + 1, QUARTERS, SUB, 256), f32),
            pltpu.VMEM((ITERS + 1, QUARTERS, SUB, 256), f32),
            pltpu.VMEM((ITERS + 1, SUB, 128), f32),
            pltpu.VMEM((ITERS + 1, SUB, 128), f32),
            pltpu.VMEM((SUB, width), bf16),
            pltpu.VMEM((CL_DEV, QUARTERS, SUB, 256), f32),
            dma, dma, dma, dma((CLUSTERS,)), dma((CLUSTERS,)), dma((CLUSTERS,)),
            dma((5 * (ITERS + 1),)), dma((5 * (ITERS + 1),)),
            dma((16,)), dma((16,)), dma((16,)), dma((16,)), dma((16,)),
        ],
        compiler_params=pltpu.CompilerParams(
            collective_id=0, has_side_effects=True, vmem_limit_bytes=56 * 2**20),
    )(points, cluster_of.reshape(1, rows), sub_init.reshape(1, rows))
    return jnp.transpose(result, (1, 0, 2))


def solution(mesh):
    in_specs = (P(("own", "help"), None), P(("own", "help"), None), P(("own", "help")))
    out_specs = P(None, "own", None)
    return jax.shard_map(shards, mesh=mesh, in_specs=in_specs, out_specs=out_specs, check_vma=False)
```

```python
import jax
import jax.numpy as jnp
from jax import lax
from jax.experimental import pallas as pl
from jax.experimental.pallas import tpu as pltpu
from jax.sharding import PartitionSpec as P

SUB = 64
ITERS = 3
CL_DEV = 4
CLUSTERS = 64
MOST = 80
GROUP = 4
WINDOW = 7
PARTS = 2
WIDE = 512

MESH = pl.DeviceIdType.MESH
NT = (((1,), (1,)), ((), ()))
f32, bf16, i32 = jnp.float32, jnp.bfloat16, jnp.int32


CODES = [
    42, 58, 16, 41, 3, 43, 1, 46, 4, 38, 12, 26, 48, 54, 28, 34, 8, 59, 17, 45, 7, 30, 52, 47, 5,
    62, 20, 37, 15, 22, 60, 10, 32, 39, 13, 40, 2, 27, 49, 57, 19, 25, 51, 61, 23, 6, 44, 50, 24,
    29, 55, 18, 56, 63, 21, 11, 33, 36, 14, 53, 31, 35, 9, 0,
]
ORDER = [(code // 16, code // 4 % 4, code % 4) for code in CODES]


def kernel(x_hbm, label_ref, init_ref, out_ref,
           x, packed, block, turned, pick, key, owner, tags, tags_in, live, weights,
           part, part_in, mass, mass_in, centre, final,
           x_sem, own_sem, send, recv, tag_send, tag_recv, part_send, part_recv,
           fin_send, fin_recv, half_send, half_recv, out_sem):
    own, hlp = lax.axis_index("own"), lax.axis_index("help")
    cx, cz, cy, core = own // 4, own % 4, hlp // 2, hlp % 2
    sign = 1 + 2 * core

    def chip(dx, dy, dz):
        return (cx + dx * sign) % 4, (cy + dy * sign) % 4, (cz + dz * sign) % 4

    def device(px, py, pz):
        return (px * 4 + pz, py * 2 + core)

    sibling = (own, cy * 2 + 1 - core)

    barrier = pltpu.get_barrier_semaphore()

    @pl.loop(1, 64)
    def _(i):
        pl.semaphore_signal(barrier, inc=1, device_id=device(*chip(i // 16, i // 4 % 4, i % 4)),
                            device_id_type=MESH)
    pl.semaphore_signal(barrier, inc=1, device_id=sibling, device_id_type=MESH)

    load = pltpu.make_async_copy(x_hbm, x, x_sem)
    load.start()

    slot_id = lax.broadcasted_iota(i32, (CLUSTERS, 1), 0)
    owners = jnp.zeros((CLUSTERS, 1), i32)
    for i, offset in enumerate(ORDER):
        px, py, pz = chip(*offset)
        cluster = px * 16 + pz * 4 + py
        owner[i] = cluster
        owners = jnp.where(slot_id == i, cluster, owners)

    rows = lax.broadcasted_iota(i32, (256, 256), 0)
    cols = lax.broadcasted_iota(i32, (256, 256), 1)
    before = (rows < cols).astype(f32).astype(bf16)
    counts = jnp.zeros((CLUSTERS, 1), f32)
    tag = jnp.zeros((CLUSTERS, 128), f32)
    for j in range(16):
        label = label_ref[:, pl.ds(j * 256, 256)]
        member = (label == owners).astype(f32)
        earlier = jnp.dot(member.astype(bf16), before, preferred_element_type=f32) + counts
        counts = counts + jnp.sum(member, axis=1, keepdims=True)
        rank = jnp.sum(member * earlier, axis=0, keepdims=True).astype(i32)
        key[:, pl.ds(j * 256, 256)] = label * 128 + rank
        at_rank = (rank == lax.broadcasted_iota(i32, (128, 256), 0)).astype(f32).astype(bf16)
        mark = (member * (init_ref[:, pl.ds(j * 256, 256)] + 1).astype(f32)).astype(bf16)
        tag = tag + lax.dot_general(mark, at_rank, NT, preferred_element_type=f32)
    for i in range(CLUSTERS):
        tags[i] = jnp.broadcast_to(tag[i:i + 1, :], (8, 128))
    tags_in[CLUSTERS - 1] = jnp.broadcast_to(tag[CLUSTERS - 1:, :], (8, 128))

    load.wait()

    def slots(i):
        return pl.ds(pl.multiple_of(i * MOST, 16), MOST)

    def rows_copy(i, target):
        return pltpu.make_async_remote_copy(
            src_ref=packed.at[slots(i)], dst_ref=block.at[slots(i)],
            send_sem=send, recv_sem=recv.at[i],
            device_id=target, device_id_type=MESH)

    def tags_copy(i, target):
        return pltpu.make_async_remote_copy(
            src_ref=tags.at[i], dst_ref=tags_in.at[i], send_sem=tag_send.at[i], recv_sem=tag_recv.at[i],
            device_id=target, device_id_type=MESH)

    groups = CLUSTERS // GROUP

    @pl.loop(0, groups + 1)
    def _(g):
        @pl.when(g == 1)
        def _():
            pl.semaphore_wait(barrier, 64)

        for n in range(GROUP):
            i = (g - 1) * GROUP + n
            code = jnp.int32(0)
            for k in range(groups):
                ox, oy, oz = ORDER[k * GROUP + n]
                code = jnp.where(g == k + 1, ox * 16 + oy * 4 + oz, code)
            target = device(*chip(code // 16, code // 4 % 4, code % 4))

            @pl.when(i >= WINDOW)
            def _():
                rows_copy(0, sibling).wait_send()

            @pl.when((i >= 0) & (i < CLUSTERS - 1))
            def _():
                tags_copy(i, target).start()
                rows_copy(i, target).start()

            @pl.when(g < groups)
            def _():
                if n == 0:
                    where = key[...]
                    for j in range(GROUP):
                        shifted = where - owner[g * GROUP + j] * 128
                        pick[pl.ds(j * MOST, MOST), :] = (
                            shifted == lax.broadcasted_iota(i32, (MOST, 1), 0)).astype(f32).astype(bf16)
                moved = jnp.dot(pick[...], x[:, n * 256:(n + 1) * 256], preferred_element_type=f32)
                start = pl.multiple_of(g * GROUP * MOST, 16)
                packed[pl.ds(start, GROUP * MOST), n * 256:(n + 1) * 256] = moved.astype(bf16)

    keep = pltpu.make_async_copy(
        packed.at[slots(CLUSTERS - 1)], block.at[slots(CLUSTERS - 1)], own_sem)
    keep.start()
    keep.wait()

    lane = lax.broadcasted_iota(i32, (128, 8 * MOST), 1)
    row = lax.broadcasted_iota(i32, (128, 8 * MOST), 0)
    spread = jnp.zeros((128, 8 * MOST), f32)
    for j in range(8):
        spread = jnp.where(lane - row == j * MOST, 1.0, spread)
    spread = jnp.where(row < MOST, spread, 0.0).astype(bf16)
    lane8 = lax.broadcasted_iota(i32, (8, 8 * MOST), 1) - MOST * lax.broadcasted_iota(i32, (8, 8 * MOST), 0)
    in_block = ((lane8 >= 0) & (lane8 < MOST)).astype(f32)
    part[0] = jnp.zeros_like(part[0])
    mass[0] = jnp.zeros_like(mass[0])

    @pl.loop(0, 8)
    def _(g):
        for j in range(8):
            i = g * 8 + j

            @pl.when(i < CLUSTERS - 1)
            def _():
                tags_copy(i, sibling).wait_recv()
                rows_copy(i, sibling).wait_recv()
        marks = tags_in[pl.ds(g * 8, 8), 0, :].astype(bf16)
        mark = jnp.sum(jnp.dot(marks, spread, preferred_element_type=f32) * in_block,
                       axis=0, keepdims=True)
        start = pl.multiple_of(g * 8 * MOST, 128)
        live[0:1, pl.ds(start, 8 * MOST)] = (mark > 0.0).astype(f32)
        chosen = (mark.astype(i32) == lax.broadcasted_iota(i32, (SUB, 1), 0) + 1).astype(f32)
        data = block[pl.ds(start, 8 * MOST), :]
        turned[:, pl.ds(start, 8 * MOST)] = data.T
        for n in range(PARTS):
            part[0, n] += jnp.dot(chosen.astype(bf16), data[:, n * WIDE:(n + 1) * WIDE],
                                  preferred_element_type=f32)
        mass[0] += sum(chosen[:, k * 128:(k + 1) * 128] for k in range(5))

    def swap(t, n):
        return pltpu.make_async_remote_copy(
            src_ref=part.at[t, n], dst_ref=part_in.at[t, n],
            send_sem=part_send.at[t * 3 + n], recv_sem=part_recv.at[t * 3 + n],
            device_id=sibling, device_id_type=MESH)

    def swap_mass(t):
        return pltpu.make_async_remote_copy(
            src_ref=mass.at[t], dst_ref=mass_in.at[t],
            send_sem=part_send.at[t * 3 + 2], recv_sem=part_recv.at[t * 3 + 2],
            device_id=sibling, device_id_type=MESH)

    def divisor(t):
        swap_mass(t).wait_recv()
        return jnp.sum(mass[t] + mass_in[t], axis=1, keepdims=True) + 1.0

    def combine(t, n, below):
        swap(t, n).wait_recv()
        current = (part[t, n] + part_in[t, n]) / below
        final[cy, n] = current
        centre[:, n * WIDE:(n + 1) * WIDE] = current.astype(bf16)
        return jnp.sum(current * current, axis=1, keepdims=True)

    half = pl.ds(core * 32, 32)

    def along(d, n):
        return pltpu.make_async_remote_copy(
            src_ref=final.at[cy, n, half], dst_ref=final.at[cy, n, half],
            send_sem=fin_send.at[d * 2 + n], recv_sem=fin_recv.at[d * 2 + n],
            device_id=(own, (cy + d) % 4 * 2 + core), device_id_type=MESH)

    def across(d, n):
        there = final.at[(cy + 4 - d) % 4, n, half]
        return pltpu.make_async_remote_copy(
            src_ref=there, dst_ref=there,
            send_sem=half_send.at[d * 2 + n], recv_sem=half_recv.at[d * 2 + n],
            device_id=sibling, device_id_type=MESH)

    def store(d, n):
        j = (cy + 4 - d) % 4
        return pltpu.make_async_copy(
            final.at[j, n], out_ref.at[j, :, pl.ds(n * WIDE, WIDE)], out_sem.at[d * 2 + n])

    swap_mass(0).start()
    for n in range(PARTS):
        swap(0, n).start()
    below = divisor(0)
    squared = jnp.zeros((SUB, 1), f32)
    for n in range(PARTS):
        squared = squared + combine(0, n, below)

    def iteration(t, squared):
        bias = squared * 0.125
        heavy = jnp.zeros((SUB, 128), f32)
        for g in range(8):
            lanes = slice(g * 8 * MOST, (g + 1) * 8 * MOST)
            product = jnp.dot(centre[...], turned[:, lanes], preferred_element_type=f32)
            score = product * 0.25 - bias
            grown = jnp.exp(score - jnp.max(score, axis=0, keepdims=True))
            weight = (grown / jnp.sum(grown, axis=0, keepdims=True) * live[0:1, lanes]).astype(bf16)
            weights[:, lanes] = weight
            wide = weight.astype(f32)
            heavy = heavy + sum(wide[:, k * 128:(k + 1) * 128] for k in range(5))
        mass[t + 1] = heavy
        swap_mass(t + 1).start()

        def finish(n, below):
            after = combine(t + 1, n, below)

            @pl.when(t == ITERS - 1)
            def _():
                for d in (1, 3, 2):
                    along(d, n).start()
            return after

        squared = jnp.zeros((SUB, 1), f32)
        for n in range(PARTS):
            part[t + 1, n] = jnp.dot(weights[...], block[:, n * WIDE:(n + 1) * WIDE],
                                     preferred_element_type=f32)
            swap(t + 1, n).start()
            if n == 0:
                below = divisor(t + 1)
            else:
                squared = squared + finish(n - 1, below)
        return squared + finish(PARTS - 1, below)

    lax.fori_loop(0, ITERS, iteration, squared)

    for n in range(PARTS):
        store(0, n).start()
    for n in range(PARTS):
        for d in (1, 3, 2):
            along(d, n).wait_recv()
            across(d, n).start()
    for n in range(PARTS):
        for d in (1, 3, 2):
            across(d, n).wait_recv()
            store(d, n).start()

    @pl.loop(0, WINDOW - 1)
    def _(k):
        rows_copy(0, sibling).wait_send()

    @pl.loop(0, CLUSTERS - 1)
    def _(i):
        tags_copy(i, sibling).wait_send()

    for t in range(ITERS + 1):
        swap_mass(t).wait_send()
        for n in range(PARTS):
            swap(t, n).wait_send()
    for n in range(PARTS):
        store(0, n).wait()
        for d in (1, 3, 2):
            along(d, n).wait_send()
            across(d, n).wait_send()
            store(d, n).wait()


def shards(points, cluster_of, sub_init):
    rows, width = points.shape
    dma = pltpu.SemaphoreType.DMA
    result = pl.pallas_call(
        kernel,
        out_shape=jax.ShapeDtypeStruct((CL_DEV, SUB, width), f32),
        in_specs=[pl.BlockSpec(memory_space=pl.ANY)] + [pl.BlockSpec(memory_space=pltpu.VMEM)] * 2,
        out_specs=pl.BlockSpec(memory_space=pl.ANY),
        scratch_shapes=[
            pltpu.VMEM((rows, width), bf16),
            pltpu.VMEM((CLUSTERS * MOST, width), bf16),
            pltpu.VMEM((CLUSTERS * MOST, width), bf16),
            pltpu.VMEM((width, CLUSTERS * MOST), bf16),
            pltpu.VMEM((GROUP * MOST, rows), bf16),
            pltpu.VMEM((1, rows), i32),
            pltpu.SMEM((CLUSTERS,), i32),
            pltpu.VMEM((CLUSTERS, 8, 128), f32),
            pltpu.VMEM((CLUSTERS, 8, 128), f32),
            pltpu.VMEM((8, CLUSTERS * MOST), f32),
            pltpu.VMEM((SUB, CLUSTERS * MOST), bf16),
            pltpu.VMEM((ITERS + 1, PARTS, SUB, WIDE), f32),
            pltpu.VMEM((ITERS + 1, PARTS, SUB, WIDE), f32),
            pltpu.VMEM((ITERS + 1, SUB, 128), f32),
            pltpu.VMEM((ITERS + 1, SUB, 128), f32),
            pltpu.VMEM((SUB, width), bf16),
            pltpu.VMEM((CL_DEV, PARTS, SUB, WIDE), f32),
            dma, dma, dma, dma((CLUSTERS,)), dma((CLUSTERS,)), dma((CLUSTERS,)),
            dma((3 * (ITERS + 1),)), dma((3 * (ITERS + 1),)),
            dma((8,)), dma((8,)), dma((8,)), dma((8,)), dma((8,)),
        ],
        compiler_params=pltpu.CompilerParams(
            collective_id=0, has_side_effects=True, vmem_limit_bytes=56 * 2**20),
    )(points, cluster_of.reshape(1, rows), sub_init.reshape(1, rows))
    return jnp.transpose(result, (1, 0, 2))


def solution(mesh):
    in_specs = (P(("own", "help"), None), P(("own", "help"), None), P(("own", "help")))
    out_specs = P(None, "own", None)
    return jax.shard_map(shards, mesh=mesh, in_specs=in_specs, out_specs=out_specs, check_vma=False)
```

```python
import jax
import jax.numpy as jnp
from jax import lax
from jax.experimental import pallas as pl
from jax.experimental.pallas import tpu as pltpu
from jax.sharding import PartitionSpec as P

SUB = 64
ITERS = 3
CL_DEV = 4
CLUSTERS = 64
MOST = 80
GROUP = 4
WINDOW = 7
PARTS = 2
WIDE = 512

MESH = pl.DeviceIdType.MESH
NT = (((1,), (1,)), ((), ()))
f32, bf16, i32 = jnp.float32, jnp.bfloat16, jnp.int32


CODES = [
    42, 58, 16, 41, 3, 43, 1, 46, 4, 38, 12, 26, 48, 54, 28, 34, 8, 59, 17, 45, 7, 30, 52, 47, 5,
    62, 20, 37, 15, 22, 60, 10, 32, 39, 13, 40, 2, 27, 49, 57, 19, 25, 51, 61, 23, 6, 44, 50, 24,
    29, 55, 18, 56, 63, 21, 11, 33, 36, 14, 53, 31, 35, 9, 0,
]
ORDER = [(code // 16, code // 4 % 4, code % 4) for code in CODES]


def kernel(x_hbm, label_ref, init_ref, out_ref,
           x, packed, block, turned, pick, key, owner, tags, tags_in, live, weights,
           part, part_in, mass, mass_in, centre, final,
           x_sem, own_sem, send, recv, tag_send, tag_recv, part_send, part_recv,
           fin_send, fin_recv, half_send, half_recv, out_sem):
    own, hlp = lax.axis_index("own"), lax.axis_index("help")
    cx, cz, cy, core = own // 4, own % 4, hlp // 2, hlp % 2
    sign = 1 + 2 * core

    def chip(dx, dy, dz):
        return (cx + dx * sign) % 4, (cy + dy * sign) % 4, (cz + dz * sign) % 4

    def device(px, py, pz):
        return (px * 4 + pz, py * 2 + core)

    sibling = (own, cy * 2 + 1 - core)

    load = pltpu.make_async_copy(x_hbm, x, x_sem)
    load.start()

    barrier = pltpu.get_barrier_semaphore()
    xs, ys, zs = ([(c + d) % 4 for d in range(4)] for c in (cx, cy, cz))
    for dx, dy, dz in sorted(ORDER[:-1], key=lambda o: -sum(min(d, 4 - d) for d in o)):
        pl.semaphore_signal(barrier, inc=1, device_id=device(xs[dx], ys[dy], zs[dz]), device_id_type=MESH)
    pl.semaphore_signal(barrier, inc=1, device_id=sibling, device_id_type=MESH)

    slot_id = lax.broadcasted_iota(i32, (CLUSTERS, 1), 0)
    owners = jnp.zeros((CLUSTERS, 1), i32)
    for i, offset in enumerate(ORDER):
        px, py, pz = chip(*offset)
        cluster = px * 16 + pz * 4 + py
        owner[i] = cluster
        owners = jnp.where(slot_id == i, cluster, owners)

    rows = lax.broadcasted_iota(i32, (256, 256), 0)
    cols = lax.broadcasted_iota(i32, (256, 256), 1)
    before = (rows < cols).astype(f32).astype(bf16)
    counts = jnp.zeros((CLUSTERS, 1), f32)
    tag = jnp.zeros((CLUSTERS, 128), f32)
    for j in range(16):
        label = label_ref[:, pl.ds(j * 256, 256)]
        member = (label == owners).astype(f32)
        earlier = jnp.dot(member.astype(bf16), before, preferred_element_type=f32) + counts
        counts = counts + jnp.sum(member, axis=1, keepdims=True)
        rank = jnp.sum(member * earlier, axis=0, keepdims=True).astype(i32)
        key[:, pl.ds(j * 256, 256)] = label * 128 + rank
        at_rank = (rank == lax.broadcasted_iota(i32, (128, 256), 0)).astype(f32).astype(bf16)
        mark = (member * (init_ref[:, pl.ds(j * 256, 256)] + 1).astype(f32)).astype(bf16)
        tag = tag + lax.dot_general(mark, at_rank, NT, preferred_element_type=f32)
    for i in range(CLUSTERS):
        tags[i] = jnp.broadcast_to(tag[i:i + 1, :], (8, 128))
    tags_in[CLUSTERS - 1] = jnp.broadcast_to(tag[CLUSTERS - 1:, :], (8, 128))

    load.wait()

    def slots(i):
        return pl.ds(pl.multiple_of(i * MOST, 16), MOST)

    def rows_copy(i, target):
        return pltpu.make_async_remote_copy(
            src_ref=packed.at[slots(i)], dst_ref=block.at[slots(i)],
            send_sem=send, recv_sem=recv.at[i],
            device_id=target, device_id_type=MESH)

    def tags_copy(i, target):
        return pltpu.make_async_remote_copy(
            src_ref=tags.at[i], dst_ref=tags_in.at[i], send_sem=tag_send.at[i], recv_sem=tag_recv.at[i],
            device_id=target, device_id_type=MESH)

    groups = CLUSTERS // GROUP

    @pl.loop(0, groups + 1)
    def _(g):
        @pl.when(g == 1)
        def _():
            pl.semaphore_wait(barrier, 64)

        for n in range(GROUP):
            i = (g - 1) * GROUP + n
            code = jnp.int32(0)
            for k in range(groups):
                ox, oy, oz = ORDER[k * GROUP + n]
                code = jnp.where(g == k + 1, ox * 16 + oy * 4 + oz, code)
            target = device(*chip(code // 16, code // 4 % 4, code % 4))

            @pl.when(i >= WINDOW)
            def _():
                rows_copy(0, sibling).wait_send()

            @pl.when((i >= 0) & (i < CLUSTERS - 1))
            def _():
                tags_copy(i, target).start()
                rows_copy(i, target).start()

            @pl.when(g < groups)
            def _():
                if n == 0:
                    where = key[...]
                    for j in range(GROUP):
                        shifted = where - owner[g * GROUP + j] * 128
                        pick[pl.ds(j * MOST, MOST), :] = (
                            shifted == lax.broadcasted_iota(i32, (MOST, 1), 0)).astype(f32).astype(bf16)
                moved = jnp.dot(pick[...], x[:, n * 256:(n + 1) * 256], preferred_element_type=f32)
                start = pl.multiple_of(g * GROUP * MOST, 16)
                packed[pl.ds(start, GROUP * MOST), n * 256:(n + 1) * 256] = moved.astype(bf16)

    keep = pltpu.make_async_copy(
        packed.at[slots(CLUSTERS - 1)], block.at[slots(CLUSTERS - 1)], own_sem)
    keep.start()
    keep.wait()

    lane = lax.broadcasted_iota(i32, (128, 8 * MOST), 1)
    row = lax.broadcasted_iota(i32, (128, 8 * MOST), 0)
    spread = jnp.zeros((128, 8 * MOST), f32)
    for j in range(8):
        spread = jnp.where(lane - row == j * MOST, 1.0, spread)
    spread = jnp.where(row < MOST, spread, 0.0).astype(bf16)
    lane8 = lax.broadcasted_iota(i32, (8, 8 * MOST), 1) - MOST * lax.broadcasted_iota(i32, (8, 8 * MOST), 0)
    in_block = ((lane8 >= 0) & (lane8 < MOST)).astype(f32)
    part[0] = jnp.zeros_like(part[0])
    mass[0] = jnp.zeros_like(mass[0])

    def turn(g):
        rows = pl.ds(pl.multiple_of(g * 8 * MOST, 128), 8 * MOST)
        turned[:, rows] = block[rows, :].T

    @pl.loop(0, 8)
    def _(g):
        @pl.when(g > 0)
        def _():
            turn(g - 1)

        for j in range(8):
            i = g * 8 + j

            @pl.when(i < CLUSTERS - 1)
            def _():
                tags_copy(i, sibling).wait_recv()
                rows_copy(i, sibling).wait_recv()
        marks = tags_in[pl.ds(g * 8, 8), 0, :].astype(bf16)
        mark = jnp.sum(jnp.dot(marks, spread, preferred_element_type=f32) * in_block,
                       axis=0, keepdims=True)
        start = pl.multiple_of(g * 8 * MOST, 128)
        live[0:1, pl.ds(start, 8 * MOST)] = (mark > 0.0).astype(f32)
        chosen = (mark.astype(i32) == lax.broadcasted_iota(i32, (SUB, 1), 0) + 1).astype(f32)
        data = block[pl.ds(start, 8 * MOST), :]
        for n in range(PARTS):
            part[0, n] += jnp.dot(chosen.astype(bf16), data[:, n * WIDE:(n + 1) * WIDE],
                                  preferred_element_type=f32)
        mass[0] += sum(chosen[:, k * 128:(k + 1) * 128] for k in range(5))

    def swap(t, n):
        return pltpu.make_async_remote_copy(
            src_ref=part.at[t, n], dst_ref=part_in.at[t, n],
            send_sem=part_send.at[t * 3 + n], recv_sem=part_recv.at[t * 3 + n],
            device_id=sibling, device_id_type=MESH)

    def swap_mass(t):
        return pltpu.make_async_remote_copy(
            src_ref=mass.at[t], dst_ref=mass_in.at[t],
            send_sem=part_send.at[t * 3 + 2], recv_sem=part_recv.at[t * 3 + 2],
            device_id=sibling, device_id_type=MESH)

    def divisor(t):
        swap_mass(t).wait_recv()
        return jnp.sum(mass[t] + mass_in[t], axis=1, keepdims=True) + 1.0

    def combine(t, n, below):
        swap(t, n).wait_recv()
        current = (part[t, n] + part_in[t, n]) / below
        final[cy, n] = current
        centre[:, n * WIDE:(n + 1) * WIDE] = current.astype(bf16)
        return jnp.sum(current * current, axis=1, keepdims=True)

    half = pl.ds(core * 32, 32)

    def along(d, n):
        return pltpu.make_async_remote_copy(
            src_ref=final.at[cy, n, half], dst_ref=final.at[cy, n, half],
            send_sem=fin_send.at[d * 2 + n], recv_sem=fin_recv.at[d * 2 + n],
            device_id=(own, (cy + d) % 4 * 2 + core), device_id_type=MESH)

    def across(d, n):
        there = final.at[(cy + 4 - d) % 4, n, half]
        return pltpu.make_async_remote_copy(
            src_ref=there, dst_ref=there,
            send_sem=half_send.at[d * 2 + n], recv_sem=half_recv.at[d * 2 + n],
            device_id=sibling, device_id_type=MESH)

    def store(d, n):
        j = (cy + 4 - d) % 4
        return pltpu.make_async_copy(
            final.at[j, n], out_ref.at[j, :, pl.ds(n * WIDE, WIDE)], out_sem.at[d * 2 + n])

    swap_mass(0).start()
    for n in range(PARTS):
        swap(0, n).start()
    turn(7)
    below = divisor(0)
    squared = jnp.zeros((SUB, 1), f32)
    for n in range(PARTS):
        squared = squared + combine(0, n, below)

    def iteration(t, squared):
        bias = squared * 0.125
        heavy = jnp.zeros((SUB, 128), f32)
        for g in range(8):
            lanes = slice(g * 8 * MOST, (g + 1) * 8 * MOST)
            product = jnp.dot(centre[...], turned[:, lanes], preferred_element_type=f32)
            score = product * 0.25 - bias
            grown = jnp.exp(score - jnp.max(score, axis=0, keepdims=True))
            weight = (grown / jnp.sum(grown, axis=0, keepdims=True) * live[0:1, lanes]).astype(bf16)
            weights[:, lanes] = weight
            wide = weight.astype(f32)
            heavy = heavy + sum(wide[:, k * 128:(k + 1) * 128] for k in range(5))
        mass[t + 1] = heavy
        swap_mass(t + 1).start()

        def finish(n, below):
            after = combine(t + 1, n, below)

            @pl.when(t == ITERS - 1)
            def _():
                for d in (2, 1, 3):
                    along(d, n).start()
            return after

        squared = jnp.zeros((SUB, 1), f32)
        for n in range(PARTS):
            part[t + 1, n] = jnp.dot(weights[...], block[:, n * WIDE:(n + 1) * WIDE],
                                     preferred_element_type=f32)
            swap(t + 1, n).start()
            if n == 0:
                below = divisor(t + 1)
            else:
                squared = squared + finish(n - 1, below)
        return squared + finish(PARTS - 1, below)

    lax.fori_loop(0, ITERS, iteration, squared)

    for n in range(PARTS):
        store(0, n).start()

    @pl.loop(0, WINDOW - 1)
    def _(k):
        rows_copy(0, sibling).wait_send()

    @pl.loop(0, CLUSTERS - 1)
    def _(i):
        tags_copy(i, sibling).wait_send()

    for t in range(ITERS + 1):
        swap_mass(t).wait_send()
        for n in range(PARTS):
            swap(t, n).wait_send()
    for n in range(PARTS):
        for d in (1, 3, 2):
            along(d, n).wait_recv()
            across(d, n).start()
    for n in range(PARTS):
        for d in (1, 3, 2):
            across(d, n).wait_recv()
            store(d, n).start()

    for n in range(PARTS):
        store(0, n).wait()
        for d in (1, 3, 2):
            along(d, n).wait_send()
            across(d, n).wait_send()
            store(d, n).wait()


def shards(points, cluster_of, sub_init):
    rows, width = points.shape
    dma = pltpu.SemaphoreType.DMA
    result = pl.pallas_call(
        kernel,
        out_shape=jax.ShapeDtypeStruct((CL_DEV, SUB, width), f32),
        in_specs=[pl.BlockSpec(memory_space=pl.ANY)] + [pl.BlockSpec(memory_space=pltpu.VMEM)] * 2,
        out_specs=pl.BlockSpec(memory_space=pl.ANY),
        scratch_shapes=[
            pltpu.VMEM((rows, width), bf16),
            pltpu.VMEM((CLUSTERS * MOST, width), bf16),
            pltpu.VMEM((CLUSTERS * MOST, width), bf16),
            pltpu.VMEM((width, CLUSTERS * MOST), bf16),
            pltpu.VMEM((GROUP * MOST, rows), bf16),
            pltpu.VMEM((1, rows), i32),
            pltpu.SMEM((CLUSTERS,), i32),
            pltpu.VMEM((CLUSTERS, 8, 128), f32),
            pltpu.VMEM((CLUSTERS, 8, 128), f32),
            pltpu.VMEM((8, CLUSTERS * MOST), f32),
            pltpu.VMEM((SUB, CLUSTERS * MOST), bf16),
            pltpu.VMEM((ITERS + 1, PARTS, SUB, WIDE), f32),
            pltpu.VMEM((ITERS + 1, PARTS, SUB, WIDE), f32),
            pltpu.VMEM((ITERS + 1, SUB, 128), f32),
            pltpu.VMEM((ITERS + 1, SUB, 128), f32),
            pltpu.VMEM((SUB, width), bf16),
            pltpu.VMEM((CL_DEV, PARTS, SUB, WIDE), f32),
            dma, dma, dma, dma((CLUSTERS,)), dma((CLUSTERS,)), dma((CLUSTERS,)),
            dma((3 * (ITERS + 1),)), dma((3 * (ITERS + 1),)),
            dma((8,)), dma((8,)), dma((8,)), dma((8,)), dma((8,)),
        ],
        compiler_params=pltpu.CompilerParams(
            collective_id=0, has_side_effects=True, vmem_limit_bytes=56 * 2**20),
    )(points, cluster_of.reshape(1, rows), sub_init.reshape(1, rows))
    return jnp.transpose(result, (1, 0, 2))


def solution(mesh):
    in_specs = (P(("own", "help"), None), P(("own", "help"), None), P(("own", "help")))
    out_specs = P(None, "own", None)
    return jax.shard_map(shards, mesh=mesh, in_specs=in_specs, out_specs=out_specs, check_vma=False)
```

```python
import jax
import jax.numpy as jnp
from jax import lax
from jax.experimental import pallas as pl
from jax.experimental.pallas import tpu as pltpu
from jax.sharding import PartitionSpec as P

SUB = 64
ITERS = 3
CL_DEV = 4
CLUSTERS = 64
MOST = 80
GROUP = 4
WINDOW = 7
PARTS = 2
WIDE = 512

MESH = pl.DeviceIdType.MESH
NT = (((1,), (1,)), ((), ()))
f32, bf16, i32 = jnp.float32, jnp.bfloat16, jnp.int32


CODES = [
    42, 58, 16, 41, 3, 43, 1, 46, 4, 38, 12, 26, 48, 54, 28, 34, 8, 59, 17, 45, 7, 30, 52, 47, 5,
    62, 20, 37, 15, 22, 60, 10, 32, 39, 13, 40, 2, 27, 49, 57, 19, 25, 51, 61, 23, 6, 44, 50, 24,
    29, 55, 18, 56, 63, 21, 11, 33, 36, 14, 53, 31, 35, 9, 0,
]
ORDER = [(code // 16, code // 4 % 4, code % 4) for code in CODES]


def kernel(x_hbm, label_ref, init_ref, out_ref,
           x, packed, block, turned, pick, key, owner, tags, tags_in, live, weights,
           part, part_in, mass, mass_in, centre, early, final,
           x_sem, own_sem, send, recv, tag_send, tag_recv, part_send, part_recv,
           fin_send, fin_recv, half_send, half_recv, out_sem):
    own, hlp = lax.axis_index("own"), lax.axis_index("help")
    cx, cz, cy, core = own // 4, own % 4, hlp // 2, hlp % 2
    sign = 1 + 2 * core

    def chip(dx, dy, dz):
        return (cx + dx * sign) % 4, (cy + dy * sign) % 4, (cz + dz * sign) % 4

    def device(px, py, pz):
        return (px * 4 + pz, py * 2 + core)

    sibling = (own, cy * 2 + 1 - core)

    load = pltpu.make_async_copy(x_hbm, x, x_sem)
    load.start()

    barrier = pltpu.get_barrier_semaphore()
    xs, ys, zs = ([(c + d) % 4 for d in range(4)] for c in (cx, cy, cz))
    for dx, dy, dz in sorted(ORDER[:-1], key=lambda o: -sum(min(d, 4 - d) for d in o)):
        pl.semaphore_signal(barrier, inc=1, device_id=device(xs[dx], ys[dy], zs[dz]), device_id_type=MESH)
    pl.semaphore_signal(barrier, inc=1, device_id=sibling, device_id_type=MESH)

    slot_id = lax.broadcasted_iota(i32, (CLUSTERS, 1), 0)
    owners = jnp.zeros((CLUSTERS, 1), i32)
    for i, offset in enumerate(ORDER):
        px, py, pz = chip(*offset)
        cluster = px * 16 + pz * 4 + py
        owner[i] = cluster
        owners = jnp.where(slot_id == i, cluster, owners)

    rows = lax.broadcasted_iota(i32, (256, 256), 0)
    cols = lax.broadcasted_iota(i32, (256, 256), 1)
    before = (rows < cols).astype(f32).astype(bf16)
    counts = jnp.zeros((CLUSTERS, 1), f32)
    tag = jnp.zeros((CLUSTERS, 128), f32)
    for j in range(16):
        label = label_ref[:, pl.ds(j * 256, 256)]
        member = (label == owners).astype(f32)
        earlier = jnp.dot(member.astype(bf16), before, preferred_element_type=f32) + counts
        counts = counts + jnp.sum(member, axis=1, keepdims=True)
        rank = jnp.sum(member * earlier, axis=0, keepdims=True).astype(i32)
        key[:, pl.ds(j * 256, 256)] = label * 128 + rank
        at_rank = (rank == lax.broadcasted_iota(i32, (128, 256), 0)).astype(f32).astype(bf16)
        mark = (member * (init_ref[:, pl.ds(j * 256, 256)] + 1).astype(f32)).astype(bf16)
        tag = tag + lax.dot_general(mark, at_rank, NT, preferred_element_type=f32)
    for i in range(CLUSTERS):
        tags[i] = jnp.broadcast_to(tag[i:i + 1, :], (8, 128))
    tags_in[CLUSTERS - 1] = jnp.broadcast_to(tag[CLUSTERS - 1:, :], (8, 128))

    load.wait()

    def slots(i):
        return pl.ds(pl.multiple_of(i * MOST, 16), MOST)

    def rows_copy(i, target):
        return pltpu.make_async_remote_copy(
            src_ref=packed.at[slots(i)], dst_ref=block.at[slots(i)],
            send_sem=send, recv_sem=recv.at[i],
            device_id=target, device_id_type=MESH)

    def tags_copy(i, target):
        return pltpu.make_async_remote_copy(
            src_ref=tags.at[i], dst_ref=tags_in.at[i], send_sem=tag_send.at[i], recv_sem=tag_recv.at[i],
            device_id=target, device_id_type=MESH)

    groups = CLUSTERS // GROUP

    @pl.loop(0, groups + 1)
    def _(g):
        @pl.when(g == 1)
        def _():
            pl.semaphore_wait(barrier, 64)

        for n in range(GROUP):
            i = (g - 1) * GROUP + n
            code = jnp.int32(0)
            for k in range(groups):
                ox, oy, oz = ORDER[k * GROUP + n]
                code = jnp.where(g == k + 1, ox * 16 + oy * 4 + oz, code)
            target = device(*chip(code // 16, code // 4 % 4, code % 4))

            @pl.when(i >= WINDOW)
            def _():
                rows_copy(0, sibling).wait_send()

            @pl.when((i >= 0) & (i < CLUSTERS - 1))
            def _():
                tags_copy(i, target).start()
                rows_copy(i, target).start()

            @pl.when(g < groups)
            def _():
                if n == 0:
                    where = key[...]
                    for j in range(GROUP):
                        shifted = where - owner[g * GROUP + j] * 128
                        pick[pl.ds(j * MOST, MOST), :] = (
                            shifted == lax.broadcasted_iota(i32, (MOST, 1), 0)).astype(f32).astype(bf16)
                moved = jnp.dot(pick[...], x[:, n * 256:(n + 1) * 256], preferred_element_type=f32)
                start = pl.multiple_of(g * GROUP * MOST, 16)
                packed[pl.ds(start, GROUP * MOST), n * 256:(n + 1) * 256] = moved.astype(bf16)

    keep = pltpu.make_async_copy(
        packed.at[slots(CLUSTERS - 1)], block.at[slots(CLUSTERS - 1)], own_sem)
    keep.start()
    keep.wait()

    lane = lax.broadcasted_iota(i32, (128, 8 * MOST), 1)
    row = lax.broadcasted_iota(i32, (128, 8 * MOST), 0)
    spread = jnp.zeros((128, 8 * MOST), f32)
    for j in range(8):
        spread = jnp.where(lane - row == j * MOST, 1.0, spread)
    spread = jnp.where(row < MOST, spread, 0.0).astype(bf16)
    lane8 = lax.broadcasted_iota(i32, (8, 8 * MOST), 1) - MOST * lax.broadcasted_iota(i32, (8, 8 * MOST), 0)
    in_block = ((lane8 >= 0) & (lane8 < MOST)).astype(f32)
    part[0] = jnp.zeros_like(part[0])
    mass[0] = jnp.zeros_like(mass[0])

    def turn(g):
        rows = pl.ds(pl.multiple_of(g * 8 * MOST, 128), 8 * MOST)
        turned[:, rows] = block[rows, :].T

    @pl.loop(0, 8)
    def _(g):
        @pl.when(g > 0)
        def _():
            turn(g - 1)

        for j in range(8):
            i = g * 8 + j

            @pl.when(i < CLUSTERS - 1)
            def _():
                tags_copy(i, sibling).wait_recv()
                rows_copy(i, sibling).wait_recv()
        marks = tags_in[pl.ds(g * 8, 8), 0, :].astype(bf16)
        mark = jnp.sum(jnp.dot(marks, spread, preferred_element_type=f32) * in_block,
                       axis=0, keepdims=True)
        start = pl.multiple_of(g * 8 * MOST, 128)
        live[0:1, pl.ds(start, 8 * MOST)] = (mark > 0.0).astype(f32)
        chosen = (mark.astype(i32) == lax.broadcasted_iota(i32, (SUB, 1), 0) + 1).astype(f32)
        data = block[pl.ds(start, 8 * MOST), :]
        for n in range(PARTS):
            part[0, n] += jnp.dot(chosen.astype(bf16), data[:, n * WIDE:(n + 1) * WIDE],
                                  preferred_element_type=f32)
        mass[0] += sum(chosen[:, k * 128:(k + 1) * 128] for k in range(5))

    def swap(t, n):
        return pltpu.make_async_remote_copy(
            src_ref=part.at[t, n], dst_ref=part_in.at[t, n],
            send_sem=part_send.at[t * 3 + n], recv_sem=part_recv.at[t * 3 + n],
            device_id=sibling, device_id_type=MESH)

    def swap_mass(t):
        return pltpu.make_async_remote_copy(
            src_ref=mass.at[t], dst_ref=mass_in.at[t],
            send_sem=part_send.at[t * 3 + 2], recv_sem=part_recv.at[t * 3 + 2],
            device_id=sibling, device_id_type=MESH)

    def divisor(t):
        swap_mass(t).wait_recv()
        return jnp.sum(mass[t] + mass_in[t], axis=1, keepdims=True) + 1.0

    def combine(t, n, below):
        swap(t, n).wait_recv()
        current = (part[t, n] + part_in[t, n]) / below
        final[cy, n] = current
        centre[:, n * WIDE:(n + 1) * WIDE] = current.astype(bf16)
        return jnp.sum(current * current, axis=1, keepdims=True)

    half = pl.ds(core * 32, 32)

    def along(d, n):
        return pltpu.make_async_remote_copy(
            src_ref=final.at[cy, n, half], dst_ref=final.at[cy, n, half],
            send_sem=fin_send.at[d * 2 + n], recv_sem=fin_recv.at[d * 2 + n],
            device_id=(own, (cy + d) % 4 * 2 + core), device_id_type=MESH)

    def across(d, n):
        there = final.at[(cy + 4 - d) % 4, n, half]
        return pltpu.make_async_remote_copy(
            src_ref=there, dst_ref=there,
            send_sem=half_send.at[d * 2 + n], recv_sem=half_recv.at[d * 2 + n],
            device_id=sibling, device_id_type=MESH)

    def store(d, n):
        j = (cy + 4 - d) % 4
        return pltpu.make_async_copy(
            final.at[j, n], out_ref.at[j, :, pl.ds(n * WIDE, WIDE)], out_sem.at[d * 2 + n])

    swap_mass(0).start()
    for n in range(PARTS):
        swap(0, n).start()
    turn(7)
    below = divisor(0)
    squared = combine(0, 0, below)

    def iteration(t, carried):
        squared, below = carried
        blocks = [slice(g * 8 * MOST, (g + 1) * 8 * MOST) for g in range(8)]
        for lanes in blocks:
            early[:, lanes] = jnp.dot(centre[:, :WIDE], turned[:WIDE, lanes], preferred_element_type=f32)
        bias = (squared + combine(t, 1, below)) * 0.125
        heavy = jnp.zeros((SUB, 128), f32)
        for lanes in blocks:
            product = early[:, lanes] + jnp.dot(
                centre[:, WIDE:], turned[WIDE:, lanes], preferred_element_type=f32)
            score = product * 0.25 - bias
            grown = jnp.exp(score - jnp.max(score, axis=0, keepdims=True))
            weight = (grown / jnp.sum(grown, axis=0, keepdims=True) * live[0:1, lanes]).astype(bf16)
            weights[:, lanes] = weight
            wide = weight.astype(f32)
            heavy = heavy + sum(wide[:, k * 128:(k + 1) * 128] for k in range(5))
        mass[t + 1] = heavy
        swap_mass(t + 1).start()
        for n in range(PARTS):
            part[t + 1, n] = jnp.dot(weights[...], block[:, n * WIDE:(n + 1) * WIDE],
                                     preferred_element_type=f32)
            swap(t + 1, n).start()
        below = divisor(t + 1)
        squared = combine(t + 1, 0, below)

        @pl.when(t == ITERS - 1)
        def _():
            for d in (2, 1, 3):
                along(d, 0).start()
        return squared, below

    squared, below = lax.fori_loop(0, ITERS, iteration, (squared, below))
    combine(ITERS, 1, below)
    for d in (2, 1, 3):
        along(d, 1).start()

    for n in range(PARTS):
        store(0, n).start()

    @pl.loop(0, WINDOW - 1)
    def _(k):
        rows_copy(0, sibling).wait_send()

    @pl.loop(0, CLUSTERS - 1)
    def _(i):
        tags_copy(i, sibling).wait_send()

    for t in range(ITERS + 1):
        swap_mass(t).wait_send()
        for n in range(PARTS):
            swap(t, n).wait_send()
    for n in range(PARTS):
        for d in (1, 3, 2):
            along(d, n).wait_recv()
            across(d, n).start()
    for n in range(PARTS):
        for d in (1, 3, 2):
            across(d, n).wait_recv()
            store(d, n).start()

    for n in range(PARTS):
        store(0, n).wait()
        for d in (1, 3, 2):
            along(d, n).wait_send()
            across(d, n).wait_send()
            store(d, n).wait()


def shards(points, cluster_of, sub_init):
    rows, width = points.shape
    dma = pltpu.SemaphoreType.DMA
    result = pl.pallas_call(
        kernel,
        out_shape=jax.ShapeDtypeStruct((CL_DEV, SUB, width), f32),
        in_specs=[pl.BlockSpec(memory_space=pl.ANY)] + [pl.BlockSpec(memory_space=pltpu.VMEM)] * 2,
        out_specs=pl.BlockSpec(memory_space=pl.ANY),
        scratch_shapes=[
            pltpu.VMEM((rows, width), bf16),
            pltpu.VMEM((CLUSTERS * MOST, width), bf16),
            pltpu.VMEM((CLUSTERS * MOST, width), bf16),
            pltpu.VMEM((width, CLUSTERS * MOST), bf16),
            pltpu.VMEM((GROUP * MOST, rows), bf16),
            pltpu.VMEM((1, rows), i32),
            pltpu.SMEM((CLUSTERS,), i32),
            pltpu.VMEM((CLUSTERS, 8, 128), f32),
            pltpu.VMEM((CLUSTERS, 8, 128), f32),
            pltpu.VMEM((8, CLUSTERS * MOST), f32),
            pltpu.VMEM((SUB, CLUSTERS * MOST), bf16),
            pltpu.VMEM((ITERS + 1, PARTS, SUB, WIDE), f32),
            pltpu.VMEM((ITERS + 1, PARTS, SUB, WIDE), f32),
            pltpu.VMEM((ITERS + 1, SUB, 128), f32),
            pltpu.VMEM((ITERS + 1, SUB, 128), f32),
            pltpu.VMEM((SUB, width), bf16),
            pltpu.VMEM((SUB, CLUSTERS * MOST), f32),
            pltpu.VMEM((CL_DEV, PARTS, SUB, WIDE), f32),
            dma, dma, dma, dma((CLUSTERS,)), dma((CLUSTERS,)), dma((CLUSTERS,)),
            dma((3 * (ITERS + 1),)), dma((3 * (ITERS + 1),)),
            dma((8,)), dma((8,)), dma((8,)), dma((8,)), dma((8,)),
        ],
        compiler_params=pltpu.CompilerParams(
            collective_id=0, has_side_effects=True, vmem_limit_bytes=56 * 2**20),
    )(points, cluster_of.reshape(1, rows), sub_init.reshape(1, rows))
    return jnp.transpose(result, (1, 0, 2))


def solution(mesh):
    in_specs = (P(("own", "help"), None), P(("own", "help"), None), P(("own", "help")))
    out_specs = P(None, "own", None)
    return jax.shard_map(shards, mesh=mesh, in_specs=in_specs, out_specs=out_specs, check_vma=False)
```

```python
import jax
import jax.numpy as jnp
from jax import lax
from jax.experimental import pallas as pl
from jax.experimental.pallas import tpu as pltpu
from jax.sharding import PartitionSpec as P

SUB = 64
ITERS = 3
CL_DEV = 4
CLUSTERS = 64
MOST = 80
GROUP = 4
WINDOW = 7
PARTS = 2
WIDE = 512

MESH = pl.DeviceIdType.MESH
NT = (((1,), (1,)), ((), ()))
f32, bf16, i32 = jnp.float32, jnp.bfloat16, jnp.int32


CODES = [
    42, 58, 16, 41, 3, 43, 1, 46, 4, 38, 12, 26, 48, 54, 28, 34, 8, 59, 17, 45, 7, 30, 52, 47, 5,
    62, 20, 37, 15, 22, 60, 10, 32, 39, 13, 40, 2, 27, 49, 57, 19, 25, 51, 61, 23, 6, 44, 50, 24,
    29, 55, 18, 56, 63, 21, 11, 33, 36, 14, 53, 31, 35, 9, 0,
]
ORDER = [(code // 16, code // 4 % 4, code % 4) for code in CODES]


def kernel(x_hbm, label_ref, init_ref, out_ref,
           x, packed, block, turned, pick, key, owner, tags, tags_in, live, weights,
           part, part_in, mass, mass_in, centre, early, final, final16,
           x_sem, own_sem, send, recv, tag_send, tag_recv, part_send, part_recv,
           fin_send, fin_recv, half_send, half_recv, out_sem):
    own, hlp = lax.axis_index("own"), lax.axis_index("help")
    cx, cz, cy, core = own // 4, own % 4, hlp // 2, hlp % 2
    sign = 1 + 2 * core

    def chip(dx, dy, dz):
        return (cx + dx * sign) % 4, (cy + dy * sign) % 4, (cz + dz * sign) % 4

    def device(px, py, pz):
        return (px * 4 + pz, py * 2 + core)

    sibling = (own, cy * 2 + 1 - core)

    load = pltpu.make_async_copy(x_hbm, x, x_sem)
    load.start()

    barrier = pltpu.get_barrier_semaphore()
    xs, ys, zs = ([(c + d) % 4 for d in range(4)] for c in (cx, cy, cz))
    for dx, dy, dz in sorted(ORDER[:-1], key=lambda o: -sum(min(d, 4 - d) for d in o)):
        pl.semaphore_signal(barrier, inc=1, device_id=device(xs[dx], ys[dy], zs[dz]), device_id_type=MESH)
    pl.semaphore_signal(barrier, inc=1, device_id=sibling, device_id_type=MESH)

    slot_id = lax.broadcasted_iota(i32, (CLUSTERS, 1), 0)
    owners = jnp.zeros((CLUSTERS, 1), i32)
    for i, offset in enumerate(ORDER):
        px, py, pz = chip(*offset)
        cluster = px * 16 + pz * 4 + py
        owner[i] = cluster
        owners = jnp.where(slot_id == i, cluster, owners)

    rows = lax.broadcasted_iota(i32, (256, 256), 0)
    cols = lax.broadcasted_iota(i32, (256, 256), 1)
    before = (rows < cols).astype(f32).astype(bf16)
    counts = jnp.zeros((CLUSTERS, 1), f32)
    tag = jnp.zeros((CLUSTERS, 128), f32)
    for j in range(16):
        label = label_ref[:, pl.ds(j * 256, 256)]
        member = (label == owners).astype(f32)
        earlier = jnp.dot(member.astype(bf16), before, preferred_element_type=f32) + counts
        counts = counts + jnp.sum(member, axis=1, keepdims=True)
        rank = jnp.sum(member * earlier, axis=0, keepdims=True).astype(i32)
        key[:, pl.ds(j * 256, 256)] = label * 128 + rank
        at_rank = (rank == lax.broadcasted_iota(i32, (128, 256), 0)).astype(f32).astype(bf16)
        mark = (member * (init_ref[:, pl.ds(j * 256, 256)] + 1).astype(f32)).astype(bf16)
        tag = tag + lax.dot_general(mark, at_rank, NT, preferred_element_type=f32)
    for i in range(CLUSTERS):
        tags[i] = jnp.broadcast_to(tag[i:i + 1, :], (8, 128))
    tags_in[CLUSTERS - 1] = jnp.broadcast_to(tag[CLUSTERS - 1:, :], (8, 128))

    load.wait()

    def slots(i):
        return pl.ds(pl.multiple_of(i * MOST, 16), MOST)

    def rows_copy(i, target):
        return pltpu.make_async_remote_copy(
            src_ref=packed.at[slots(i)], dst_ref=block.at[slots(i)],
            send_sem=send, recv_sem=recv.at[i],
            device_id=target, device_id_type=MESH)

    def tags_copy(i, target):
        return pltpu.make_async_remote_copy(
            src_ref=tags.at[i], dst_ref=tags_in.at[i], send_sem=tag_send.at[i], recv_sem=tag_recv.at[i],
            device_id=target, device_id_type=MESH)

    groups = CLUSTERS // GROUP

    @pl.loop(0, groups + 1)
    def _(g):
        @pl.when(g == 1)
        def _():
            pl.semaphore_wait(barrier, 64)

        for n in range(GROUP):
            i = (g - 1) * GROUP + n
            code = jnp.int32(0)
            for k in range(groups):
                ox, oy, oz = ORDER[k * GROUP + n]
                code = jnp.where(g == k + 1, ox * 16 + oy * 4 + oz, code)
            target = device(*chip(code // 16, code // 4 % 4, code % 4))

            @pl.when(i >= WINDOW)
            def _():
                rows_copy(0, sibling).wait_send()

            @pl.when((i >= 0) & (i < CLUSTERS - 1))
            def _():
                tags_copy(i, target).start()
                rows_copy(i, target).start()

            @pl.when(g < groups)
            def _():
                if n == 0:
                    where = key[...]
                    for j in range(GROUP):
                        shifted = where - owner[g * GROUP + j] * 128
                        pick[pl.ds(j * MOST, MOST), :] = (
                            shifted == lax.broadcasted_iota(i32, (MOST, 1), 0)).astype(f32).astype(bf16)
                moved = jnp.dot(pick[...], x[:, n * 256:(n + 1) * 256], preferred_element_type=f32)
                start = pl.multiple_of(g * GROUP * MOST, 16)
                packed[pl.ds(start, GROUP * MOST), n * 256:(n + 1) * 256] = moved.astype(bf16)

    keep = pltpu.make_async_copy(
        packed.at[slots(CLUSTERS - 1)], block.at[slots(CLUSTERS - 1)], own_sem)
    keep.start()
    keep.wait()

    lane = lax.broadcasted_iota(i32, (128, 8 * MOST), 1)
    row = lax.broadcasted_iota(i32, (128, 8 * MOST), 0)
    spread = jnp.zeros((128, 8 * MOST), f32)
    for j in range(8):
        spread = jnp.where(lane - row == j * MOST, 1.0, spread)
    spread = jnp.where(row < MOST, spread, 0.0).astype(bf16)
    lane8 = lax.broadcasted_iota(i32, (8, 8 * MOST), 1) - MOST * lax.broadcasted_iota(i32, (8, 8 * MOST), 0)
    in_block = ((lane8 >= 0) & (lane8 < MOST)).astype(f32)
    part[0] = jnp.zeros_like(part[0])
    mass[0] = jnp.zeros_like(mass[0])

    def turn(g):
        rows = pl.ds(pl.multiple_of(g * 8 * MOST, 128), 8 * MOST)
        turned[:, rows] = block[rows, :].T

    @pl.loop(0, 8)
    def _(g):
        @pl.when(g > 0)
        def _():
            turn(g - 1)

        for j in range(8):
            i = g * 8 + j

            @pl.when(i < CLUSTERS - 1)
            def _():
                tags_copy(i, sibling).wait_recv()
                rows_copy(i, sibling).wait_recv()
        marks = tags_in[pl.ds(g * 8, 8), 0, :].astype(bf16)
        mark = jnp.sum(jnp.dot(marks, spread, preferred_element_type=f32) * in_block,
                       axis=0, keepdims=True)
        start = pl.multiple_of(g * 8 * MOST, 128)
        live[0:1, pl.ds(start, 8 * MOST)] = (mark > 0.0).astype(f32)
        chosen = (mark.astype(i32) == lax.broadcasted_iota(i32, (SUB, 1), 0) + 1).astype(f32)
        data = block[pl.ds(start, 8 * MOST), :]
        for n in range(PARTS):
            part[0, n] += jnp.dot(chosen.astype(bf16), data[:, n * WIDE:(n + 1) * WIDE],
                                  preferred_element_type=f32)
        mass[0] += sum(chosen[:, k * 128:(k + 1) * 128] for k in range(5))

    def swap(t, n):
        return pltpu.make_async_remote_copy(
            src_ref=part.at[t, n], dst_ref=part_in.at[t, n],
            send_sem=part_send.at[t * 3 + n], recv_sem=part_recv.at[t * 3 + n],
            device_id=sibling, device_id_type=MESH)

    def swap_mass(t):
        return pltpu.make_async_remote_copy(
            src_ref=mass.at[t], dst_ref=mass_in.at[t],
            send_sem=part_send.at[t * 3 + 2], recv_sem=part_recv.at[t * 3 + 2],
            device_id=sibling, device_id_type=MESH)

    def divisor(t):
        swap_mass(t).wait_recv()
        return jnp.sum(mass[t] + mass_in[t], axis=1, keepdims=True) + 1.0

    def combine(t, n, below):
        swap(t, n).wait_recv()
        current = (part[t, n] + part_in[t, n]) / below
        current16 = current.astype(bf16)
        final16[cy, n] = current16
        centre[:, n * WIDE:(n + 1) * WIDE] = current16
        return jnp.sum(current * current, axis=1, keepdims=True)

    half = pl.ds(core * 32, 32)

    def along(d, n):
        return pltpu.make_async_remote_copy(
            src_ref=final16.at[cy, n, half], dst_ref=final16.at[cy, n, half],
            send_sem=fin_send.at[d * 2 + n], recv_sem=fin_recv.at[d * 2 + n],
            device_id=(own, (cy + d) % 4 * 2 + core), device_id_type=MESH)

    def across(d, n):
        there = final16.at[(cy + 4 - d) % 4, n, half]
        return pltpu.make_async_remote_copy(
            src_ref=there, dst_ref=there,
            send_sem=half_send.at[d * 2 + n], recv_sem=half_recv.at[d * 2 + n],
            device_id=sibling, device_id_type=MESH)

    def widen(d, n):
        final[d, n] = final16[(cy + 4 - d) % 4, n].astype(f32)

    def store(d, n):
        j = (cy + 4 - d) % 4
        return pltpu.make_async_copy(
            final.at[d, n], out_ref.at[j, :, pl.ds(n * WIDE, WIDE)], out_sem.at[d * 2 + n])

    swap_mass(0).start()
    for n in range(PARTS):
        swap(0, n).start()
    turn(7)
    below = divisor(0)
    squared = combine(0, 0, below)

    def iteration(t, carried):
        squared, below = carried
        blocks = [slice(g * 8 * MOST, (g + 1) * 8 * MOST) for g in range(8)]
        for lanes in blocks:
            early[:, lanes] = jnp.dot(centre[:, :WIDE], turned[:WIDE, lanes], preferred_element_type=f32)
        bias = (squared + combine(t, 1, below)) * 0.125
        heavy = jnp.zeros((SUB, 128), f32)
        for lanes in blocks:
            product = early[:, lanes] + jnp.dot(
                centre[:, WIDE:], turned[WIDE:, lanes], preferred_element_type=f32)
            score = product * 0.25 - bias
            grown = jnp.exp(score - jnp.max(score, axis=0, keepdims=True))
            weight = (grown / jnp.sum(grown, axis=0, keepdims=True) * live[0:1, lanes]).astype(bf16)
            weights[:, lanes] = weight
            wide = weight.astype(f32)
            heavy = heavy + sum(wide[:, k * 128:(k + 1) * 128] for k in range(5))
        mass[t + 1] = heavy
        swap_mass(t + 1).start()
        for n in range(PARTS):
            part[t + 1, n] = jnp.dot(weights[...], block[:, n * WIDE:(n + 1) * WIDE],
                                     preferred_element_type=f32)
            swap(t + 1, n).start()
        below = divisor(t + 1)
        squared = combine(t + 1, 0, below)

        @pl.when(t == ITERS - 1)
        def _():
            for d in (2, 1, 3):
                along(d, 0).start()
        return squared, below

    squared, below = lax.fori_loop(0, ITERS, iteration, (squared, below))
    combine(ITERS, 1, below)
    for d in (2, 1, 3):
        along(d, 1).start()

    for n in range(PARTS):
        widen(0, n)
        store(0, n).start()

    @pl.loop(0, WINDOW - 1)
    def _(k):
        rows_copy(0, sibling).wait_send()

    @pl.loop(0, CLUSTERS - 1)
    def _(i):
        tags_copy(i, sibling).wait_send()

    for t in range(ITERS + 1):
        swap_mass(t).wait_send()
        for n in range(PARTS):
            swap(t, n).wait_send()
    for n in range(PARTS):
        for d in (1, 3, 2):
            along(d, n).wait_recv()
            across(d, n).start()
    for n in range(PARTS):
        for d in (1, 3, 2):
            across(d, n).wait_recv()
            widen(d, n)
            store(d, n).start()

    for n in range(PARTS):
        store(0, n).wait()
        for d in (1, 3, 2):
            along(d, n).wait_send()
            across(d, n).wait_send()
            store(d, n).wait()


def shards(points, cluster_of, sub_init):
    rows, width = points.shape
    dma = pltpu.SemaphoreType.DMA
    result = pl.pallas_call(
        kernel,
        out_shape=jax.ShapeDtypeStruct((CL_DEV, SUB, width), f32),
        in_specs=[pl.BlockSpec(memory_space=pl.ANY)] + [pl.BlockSpec(memory_space=pltpu.VMEM)] * 2,
        out_specs=pl.BlockSpec(memory_space=pl.ANY),
        scratch_shapes=[
            pltpu.VMEM((rows, width), bf16),
            pltpu.VMEM((CLUSTERS * MOST, width), bf16),
            pltpu.VMEM((CLUSTERS * MOST, width), bf16),
            pltpu.VMEM((width, CLUSTERS * MOST), bf16),
            pltpu.VMEM((GROUP * MOST, rows), bf16),
            pltpu.VMEM((1, rows), i32),
            pltpu.SMEM((CLUSTERS,), i32),
            pltpu.VMEM((CLUSTERS, 8, 128), f32),
            pltpu.VMEM((CLUSTERS, 8, 128), f32),
            pltpu.VMEM((8, CLUSTERS * MOST), f32),
            pltpu.VMEM((SUB, CLUSTERS * MOST), bf16),
            pltpu.VMEM((ITERS + 1, PARTS, SUB, WIDE), f32),
            pltpu.VMEM((ITERS + 1, PARTS, SUB, WIDE), f32),
            pltpu.VMEM((ITERS + 1, SUB, 128), f32),
            pltpu.VMEM((ITERS + 1, SUB, 128), f32),
            pltpu.VMEM((SUB, width), bf16),
            pltpu.VMEM((SUB, CLUSTERS * MOST), f32),
            pltpu.VMEM((CL_DEV, PARTS, SUB, WIDE), f32),
            pltpu.VMEM((CL_DEV, PARTS, SUB, WIDE), bf16),
            dma, dma, dma, dma((CLUSTERS,)), dma((CLUSTERS,)), dma((CLUSTERS,)),
            dma((3 * (ITERS + 1),)), dma((3 * (ITERS + 1),)),
            dma((8,)), dma((8,)), dma((8,)), dma((8,)), dma((8,)),
        ],
        compiler_params=pltpu.CompilerParams(
            collective_id=0, has_side_effects=True, vmem_limit_bytes=56 * 2**20),
    )(points, cluster_of.reshape(1, rows), sub_init.reshape(1, rows))
    return jnp.transpose(result, (1, 0, 2))


def solution(mesh):
    in_specs = (P(("own", "help"), None), P(("own", "help"), None), P(("own", "help")))
    out_specs = P(None, "own", None)
    return jax.shard_map(shards, mesh=mesh, in_specs=in_specs, out_specs=out_specs, check_vma=False)
```
